768 devices in a mesh: event: 16 (over y_hi, x), gx: 4 (over y_lo, core), gy: 12 (over z).
Axes of the slice: x: 4, y: 8 (y_hi: 4, y_lo: 2; y = y_hi * 2 + y_lo), z: 12, core: 2. Of those that a mesh axis runs over, the one named last changes fastest.
Arguments:
- forward_prev: float32 [16, 3, 64, 192, 128], P('event', None, 'gx', 'gy'), may hold values from -6 to 6
- forward_now: float32 [16, 3, 64, 192, 128], P('event', None, 'gx', 'gy'), may hold values from -6 to 6
- born_prev: float32 [16, 3, 64, 192, 128], P('event', None, 'gx', 'gy'), may hold values from -6 to 6
- born_now: float32 [16, 3, 64, 192, 128], P('event', None, 'gx', 'gy'), may hold values from -6 to 6
- adjoint_now: float32 [16, 3, 64, 192, 128], P('event', None, 'gx', 'gy'), may hold values from -6 to 6
- adjoint_next: float32 [16, 3, 64, 192, 128], P('event', None, 'gx', 'gy'), may hold values from -6 to 6
- shear_pert: float32 [64, 192, 128], P('gx', 'gy'), may hold values from -3 to 3
- lame_depth: float32 [128], replicated, may hold values from 0.5 to 2
- shear_depth: float32 [128], replicated, may hold values from 0.3 to 1.5
- buoyancy: float32 [128], replicated, may hold values from 0.5 to 2
- drm_cells: int32 [4, 12, 1024], P('gx', 'gy'), may hold values from 124 to 32767, as said below
- drm_matrix: float32 [3, 3, 4, 12, 1024], P(None, None, 'gx', 'gy'), may hold values from -12 to 12
- drm_motion: float32 [16, 3, 4, 12, 1024], P('event', None, 'gx', 'gy'), may hold values from -6 to 6
- source_cell: int32 [16], P('event'), may hold values from 0 to 1572863
- source_force: float32 [16, 3], P('event'), may hold values from -16 to 16
Outputs:
- hess_vec: float32 [64, 192, 128], P('gx', 'gy')
- forward_next: float32 [16, 3, 64, 192, 128], P('event', None, 'gx', 'gy')
- born_next: float32 [16, 3, 64, 192, 128], P('event', None, 'gx', 'gy')
- adjoint_prev: float32 [16, 3, 64, 192, 128], P('event', None, 'gx', 'gy')
The draws below stay inside these ranges and needn't reach their ends.
Inputs may be any that keep to these rules, and one draw needn't show every extreme that they name: `drm_cells`: the 1024 entries of one tile are its distinct cells of the bottom 4 depth planes, each as (x * 16 + y) * 128 + z within the tile, in an order drawn from the seed.
All inputs are finite; a program needn't handle non-finite values.
Results may differ from the reference program's by a relative error of at most 0.0001.
Values sent between devices are 32-bit elements; how exact they have to be, the bound alone decides.
No kernel may reach another device: no remote copies, remote signals or barrier semaphores. Data moves between devices by JAX's collectives and lax.ppermute only.
A program may use at most 64 MiB of HBM per device.

```python
import math
import jax
import jax.numpy as jnp
from jax import lax

CX = 16
CY = 16
CZ = 128
LAYER = 4
EVENTS = 16
NX = 64
NY = 192
NZ = 128
TX = 4
TY = 12
ELEMS = 1024


def draw_drm_cells(key, part):
    subkeys = jax.random.split(jax.random.fold_in(key, 7), TX * TY)
    shuffled = jax.vmap(lambda single: jax.random.permutation(single, ELEMS))(subkeys)
    shuffled = shuffled.reshape(TX, TY, ELEMS).astype(jnp.int32)
    slot_x = shuffled // (CY * LAYER)
    slot_y = shuffled // LAYER % CY
    slot_z = CZ - LAYER + shuffled % LAYER
    return ((slot_x * CY + slot_y) * CZ + slot_z).astype(jnp.int32)


def set_ends(array, stream_key, smallest, largest):
    longest = array.shape.index(max(array.shape))
    spots = []
    for shift in (0, 1):
        where = [jax.random.randint(jax.random.fold_in(stream_key, axis), (), 0, length) for axis, length in enumerate(array.shape)]
        where[longest] = (where[longest] + shift) % array.shape[longest]
        spots.append(tuple(where))
    return array.at[spots[0]].set(smallest).at[spots[1]].set(largest)


def steps_of(stream_key, shape, pieces, low, top_value):
    def one(position, parts):
        steps = jax.random.uniform(jax.random.fold_in(jax.random.fold_in(stream_key, 6), position), (parts,), jnp.float32, low / len(pieces), top_value / len(pieces))
        return jnp.repeat(jnp.exp(steps), shape[position] // parts).reshape((-1,) + (1,) * (len(shape) - position - 1))

    level = one(*pieces[0])
    for cut in pieces[1:]:
        level = level * one(*cut)
    return level


def scatter_about(own_key, extent, spread, most, cuts=(), held_as=jnp.bfloat16):
    result = jax.random.normal(own_key, extent, jnp.float32) * spread
    if len(cuts) > 0:
        result = steps_of(own_key, extent, cuts, -0.22, 0.18) * result
    return jnp.clip(result, min=-most, max=most).astype(held_as)


def setup_inputs(seed: int = 0) -> dict:
    key_list = jax.random.split(jax.random.key(seed), 16)
    return {
        "forward_prev": scatter_about(key_list[0], (EVENTS, 3, NX, NY, NZ), 1.0, 6.0, ((0, 16), (2, 4), (3, 12)), jnp.float32),
        "forward_now": scatter_about(key_list[1], (EVENTS, 3, NX, NY, NZ), 1.0, 6.0, ((0, 16), (2, 4), (3, 12)), jnp.float32),
        "born_prev": scatter_about(key_list[2], (EVENTS, 3, NX, NY, NZ), 1.0, 6.0, ((0, 16), (2, 4), (3, 12)), jnp.float32),
        "born_now": scatter_about(key_list[3], (EVENTS, 3, NX, NY, NZ), 1.0, 6.0, ((0, 16), (2, 4), (3, 12)), jnp.float32),
        "adjoint_now": scatter_about(key_list[4], (EVENTS, 3, NX, NY, NZ), 1.0, 6.0, ((0, 16), (2, 4), (3, 12)), jnp.float32),
        "adjoint_next": scatter_about(key_list[5], (EVENTS, 3, NX, NY, NZ), 1.0, 6.0, ((0, 16), (2, 4), (3, 12)), jnp.float32),
        "shear_pert": scatter_about(key_list[6], (NX, NY, NZ), 0.5, 3.0, ((0, 4), (1, 12)), jnp.float32),
        "lame_depth": jnp.clip(jnp.exp(jax.random.uniform(key_list[7], (NZ,), jnp.float32, math.log(0.5), math.log(2.0))), 0.5, 2.0),
        "shear_depth": jnp.clip(jnp.exp(jax.random.uniform(key_list[8], (NZ,), jnp.float32, math.log(0.3), math.log(1.5))), 0.3, 1.5),
        "buoyancy": jnp.clip(jnp.exp(jax.random.uniform(key_list[9], (NZ,), jnp.float32, math.log(0.5), math.log(2.0))), 0.5, 2.0),
        "drm_cells": draw_drm_cells(jax.random.fold_in(key_list[15], 71), 0),
        "drm_matrix": scatter_about(key_list[11], (3, 3, TX, TY, ELEMS), 2.0, 12.0, ((2, 4), (3, 12)), jnp.float32),
        "drm_motion": scatter_about(key_list[12], (EVENTS, 3, TX, TY, ELEMS), 1.0, 6.0, ((0, 16), (2, 4), (3, 12)), jnp.float32),
        "source_cell": set_ends(jax.random.randint(key_list[13], (EVENTS,), 0, NX * NY * NZ), jax.random.fold_in(key_list[13], 1), 0, (NX * NY * NZ) - 1).astype(jnp.int32),
        "source_force": scatter_about(key_list[14], (EVENTS, 3), 4.0, 16.0, ((0, 16),), jnp.float32),
    }


def depth_derivative(interior):
    padded_z = jnp.pad(interior, [(0, 0)] * (interior.ndim - 1) + [(1, 1)])
    return (padded_z[..., 2:] - padded_z[..., :-2]) * 0.5


def gradient(padded):
    along_x = (padded[..., 2:, 1:-1, :] - padded[..., :-2, 1:-1, :]) * 0.5
    along_y = (padded[..., 1:-1, 2:, :] - padded[..., 1:-1, :-2, :]) * 0.5
    along_z = depth_derivative(padded[..., 1:-1, 1:-1, :])
    return jnp.stack([along_x, along_y, along_z], axis=-4)


def strain_pairs(gradients):
    def component(left_index, right_index):
        return gradients[..., left_index, right_index, :, :, :]

    return jnp.stack([component(0, 0) + component(0, 0), component(1, 1) + component(1, 1),
                      component(2, 2) + component(2, 2), component(0, 1) + component(1, 0),
                      component(0, 2) + component(2, 0), component(1, 2) + component(2, 1)], axis=-4)


def stress(gradients, lame_depth, shear_depth):
    strain_sums = strain_pairs(gradients)
    trace_sum = gradients[..., 0, 0, :, :, :] + gradients[..., 1, 1, :, :, :] + gradients[..., 2, 2, :, :, :]
    normal_part = lame_depth * trace_sum
    return jnp.concatenate([shear_depth * strain_sums[..., :3, :, :, :] + normal_part[..., None, :, :, :],
                            shear_depth * strain_sums[..., 3:, :, :, :]], axis=-4)


def divergence(padded):
    def along_x(member):
        return (padded[..., member, 2:, 1:-1, :] - padded[..., member, :-2, 1:-1, :]) * 0.5

    def along_y(member):
        return (padded[..., member, 1:-1, 2:, :] - padded[..., member, 1:-1, :-2, :]) * 0.5

    def along_z(member):
        return depth_derivative(padded[..., member, 1:-1, 1:-1, :])

    force_x = along_x(0) + along_y(3) + along_z(4)
    force_y = along_x(3) + along_y(1) + along_z(5)
    force_z = along_x(4) + along_y(5) + along_z(2)
    return jnp.stack([force_x, force_y, force_z], axis=-4)


def lateral_pad(field):
    return jnp.pad(field, [(0, 0)] * (field.ndim - 3) + [(1, 1), (1, 1), (0, 0)])


def reference(forward_prev, forward_now, born_prev, born_now, adjoint_now, adjoint_next, shear_pert,
              lame_depth, shear_depth, buoyancy, drm_cells, drm_matrix, drm_motion, source_cell, source_force):
    tile_x = jnp.arange(TX, dtype=jnp.int32)[:, None, None]
    tile_y = jnp.arange(TY, dtype=jnp.int32)[None, :, None]
    global_x = tile_x * CX + drm_cells // (CY * CZ)
    global_y = tile_y * CY + (drm_cells // CZ) % CY
    global_z = drm_cells % CZ
    drm_flat = ((global_x * NY + global_y) * NZ + global_z).reshape(-1).astype(jnp.int32)
    depth_scale = 0.1 * buoyancy
    surface = jnp.arange(NZ) == 0

    def event_step(running, inputs):
        forward_old, forward_mid, born_old, born_mid, adjoint_mid, adjoint_new, motion, event_cell, point_force = inputs
        fields = jnp.stack([forward_mid, born_mid, adjoint_mid])
        gradients = gradient(lateral_pad(fields))
        stresses = stress(gradients, lame_depth, shear_depth)
        born_stress = stresses[1] + shear_pert * strain_pairs(gradients[0])
        stresses = jnp.stack([stresses[0], born_stress, stresses[2]])
        forces = divergence(lateral_pad(stresses))
        element_force = jnp.sum(drm_matrix * motion[None], axis=1)
        drm_force = jnp.zeros((3, NX * NY * NZ), jnp.float32).at[:, drm_flat].add(element_force.reshape(3, -1))
        point_term = jnp.zeros((3, NX * NY * NZ), jnp.float32).at[:, event_cell].add(point_force)
        applied = (drm_force + point_term).reshape(3, NX, NY, NZ)
        forward_next = 2.0 * forward_mid - forward_old + depth_scale * (forces[0] + applied)
        born_next = 2.0 * born_mid - born_old + depth_scale * forces[1]
        received = jnp.where(surface, born_next, 0.0)
        adjoint_prev = 2.0 * adjoint_mid - adjoint_new + depth_scale * (forces[2] + received)
        final_gradients = gradient(lateral_pad(jnp.stack([forward_next, adjoint_prev])))
        paired = final_gradients[0] + jnp.swapaxes(final_gradients[0], 0, 1)
        product = jnp.sum(paired * final_gradients[1], axis=(0, 1))
        return running + (-0.05) * product, (forward_next, born_next, adjoint_prev)

    start = jnp.zeros((NX, NY, NZ), jnp.float32)
    hess_vec, outputs = lax.scan(event_step, start,
                                 (forward_prev, forward_now, born_prev, born_now, adjoint_now, adjoint_next,
                                  drm_motion, source_cell, source_force))
    return (hess_vec, outputs[0], outputs[1], outputs[2])
```

```python
import jax
import jax.numpy as jnp
from jax import lax
from jax.experimental import pallas as pl
from jax.experimental.pallas import tpu as pltpu
from jax.sharding import PartitionSpec as P

X = 16
Y = 16
Z = 128
CELLS = X * Y
LAYER = 4
ELEMS = CELLS * LAYER

Y_BASE = 27
Y_PERT = 33
Y_PLANES = 35

X_STEP = 54
X_PERT = 9 * X_STEP
X_BASE = X_PERT + 34
X_ROWS = X_BASE + 6 * Y

ROWS = 32
ZERO = 8

F32 = jnp.float32


def now_row(c, d):
    return c * X_STEP + (0, 20, 38)[d - 1]


def pert_row(d):
    return X_PERT + (0, 18)[d - 1]


def near_x(high, d):
    return jnp.where(high, X - d, d - 1)


def begin_kernel(
    place_ref,
    *refs,
):
    sources, refs = refs[:13], refs[13:]
    base_ref, low_ref, high_ref, xa_ref, xb_ref, applied_ref = refs[:6]
    held, arrived = refs[6:19], refs[19]
    copies = [
        pltpu.make_async_copy(source, ref, arrived.at[i])
        for i, (source, ref) in enumerate(zip(sources, held))
    ]
    for i in (8, 9, 10, 11, 12, 7, 6, 0, 1, 2, 3, 4, 5):
        copies[i].start()
    fprev_ref, fnow_ref, bprev_ref, bnow_ref, anow_ref, anext_ref = held[:6]
    pert_ref, buoy_ref, cells_ref, matrix_ref, motion_ref, cell_ref, force_ref = held[6:]
    for i in (8, 9, 10, 11, 12):
        copies[i].wait()

    index_x = place_ref[0]
    index_y = place_ref[1]
    total_y = place_ref[2]

    cells = cells_ref[...].reshape(1, ELEMS)
    column = cells // Z
    depth = cells % Z
    pick = jnp.where(
        lax.broadcasted_iota(jnp.int32, (CELLS, ELEMS), 0) == column, 1.0, 0.0
    ).astype(jnp.bfloat16)
    slot = lax.broadcasted_iota(jnp.int32, (16, ELEMS), 0)
    spread = jnp.zeros((16, ELEMS), F32)
    for i in range(3):
        element = sum(
            matrix_ref[3 * i + c].reshape(1, ELEMS) * motion_ref[c].reshape(1, ELEMS)
            for c in range(3)
        )
        spread = jnp.where(slot == depth - (Z - 16) - 4 * i, element, spread)
    spread = jnp.concatenate([jnp.zeros((Z - 16, ELEMS), F32), spread], axis=0)
    placed = jnp.zeros((CELLS, Z), F32)
    rest = spread
    for _ in range(3):
        part = rest.astype(jnp.bfloat16)
        placed = placed + lax.dot_general(
            pick, part, (((1,), (1,)), ((), ())), preferred_element_type=F32
        )
        rest = rest - part.astype(F32)
    lane = lax.broadcasted_iota(jnp.int32, (CELLS, Z), 1)
    for i in range(3):
        moved = placed if i == 0 else pltpu.roll(placed, 4 * i, 1)
        applied_ref[i] = jnp.where(lane >= Z - LAYER, moved, 0.0)

    cell = cell_ref[0]
    local_x = cell // (total_y * Z) - index_x * X
    local_y = (cell // Z) % total_y - index_y * Y
    inside = (local_x >= 0) & (local_x < X) & (local_y >= 0) & (local_y < Y)

    @pl.when(inside)
    def _():
        row = local_x * Y + local_y
        here = lax.broadcasted_iota(jnp.int32, (1, Z), 1) == cell % Z
        for i in range(3):
            old = applied_ref[i, pl.ds(row, 1), :]
            applied_ref[i, pl.ds(row, 1), :] = old + jnp.where(here, force_ref[:, i : i + 1], 0.0)

    for i in (7, 6, 0, 1, 2, 3, 4, 5):
        copies[i].wait()
    scale = 0.1 * buoy_ref[...].reshape(1, Z)
    surface_scale = jnp.where(lane[:1] == 0, scale, 0.0)
    for i in range(3):
        base_ref[i] = 2.0 * fnow_ref[i] - fprev_ref[i] + scale * applied_ref[i]
        born = 2.0 * bnow_ref[i] - bprev_ref[i]
        base_ref[3 + i] = born
        base_ref[6 + i] = 2.0 * anow_ref[i] - anext_ref[i] + surface_scale * born

    now = [r.at[i] for r in (fnow_ref, bnow_ref, anow_ref) for i in range(3)]
    bases = [base_ref.at[i] for i in (0, 1, 2, 6, 7, 8)]

    def column_of(ref, y):
        return ref[pl.ds(y, X, stride=Y), :]

    for c in range(9):
        for k in range(3):
            low_ref[3 * c + k] = column_of(now[c], k)
            high_ref[3 * c + k] = column_of(now[c], Y - 3 + k)
    for c in range(6):
        low_ref[Y_BASE + c] = column_of(bases[c], 0)
        high_ref[Y_BASE + c] = column_of(bases[c], Y - 1)
    for k in range(2):
        low_ref[Y_PERT + k] = column_of(pert_ref, k)
        high_ref[Y_PERT + k] = column_of(pert_ref, Y - 2 + k)

    odd = index_x % 2 == 1
    for ref, high in ((xa_ref, jnp.logical_not(odd)), (xb_ref, odd)):

        def plane_of(source, d):
            start = pl.multiple_of(near_x(high, d) * Y, Y)
            return source[pl.ds(start, Y), :]

        for c in range(9):
            for d in (1, 2, 3):
                ref[pl.ds(now_row(c, d) + 3 - d, Y), :] = plane_of(now[c], d)
        for d in (1, 2):
            ref[pl.ds(pert_row(d) + 2 - d, Y), :] = plane_of(pert_ref, d)
        for c in range(6):
            ref[pl.ds(X_BASE + c * Y, Y), :] = plane_of(bases[c], 1)


def widen_kernel(place_ref, xa_in, xb_in, left_ref, right_ref, xa_ref, xb_ref):
    odd = place_ref[0] % 2 == 1
    for source, ref, high in ((xa_in, xa_ref, jnp.logical_not(odd)), (xb_in, xb_ref, odd)):
        ref[...] = source[...]
        for d in (1, 2):
            x = near_x(high, d)
            for c in range(9):
                start = now_row(c, d)
                for k in range(3 - d):
                    ref[pl.ds(start + k, 1), :] = left_ref[3 * c + d + k, pl.ds(x, 1), :]
                    ref[pl.ds(start + 19 - d + k, 1), :] = right_ref[3 * c + k, pl.ds(x, 1), :]
        x = near_x(high, 1)
        ref[pl.ds(pert_row(1), 1), :] = left_ref[Y_PERT + 1, pl.ds(x, 1), :]
        ref[pl.ds(pert_row(1) + 17, 1), :] = right_ref[Y_PERT, pl.ds(x, 1), :]


def step_kernel(
    place_ref,
    fnow_ref,
    bnow_ref,
    anow_ref,
    pert_in,
    base_ref,
    left_ref,
    right_ref,
    xa_ref,
    xb_ref,
    lame_ref,
    shear_ref,
    buoy_ref,
    hess_ref,
    fnext_ref,
    bnext_ref,
    aprev_ref,
    wide,
    pert,
    stress,
    new,
):
    index_x = place_ref[0]
    index_y = place_ref[1]
    last_x = place_ref[3] - 1
    last_y = place_ref[4] - 1

    now = [r.at[i] for r in (fnow_ref, bnow_ref, anow_ref) for i in range(3)]
    for c in range(9):
        for x in range(X):
            wide[c, pl.ds((x + 3) * ROWS + ZERO, Y), :] = now[c][pl.ds(x * Y, Y), :]
        for k in range(3):
            wide[c, pl.ds(3 * ROWS + ZERO - 3 + k, X, stride=ROWS), :] = left_ref[3 * c + k]
            wide[c, pl.ds(3 * ROWS + ZERO + Y + k, X, stride=ROWS), :] = right_ref[3 * c + k]
    for x in range(X):
        pert[pl.ds((x + 2) * ROWS + ZERO, Y), :] = pert_in[pl.ds(x * Y, Y), :]
    for k in range(2):
        pert[pl.ds(2 * ROWS + ZERO - 2 + k, X, stride=ROWS), :] = left_ref[Y_PERT + k]
        pert[pl.ds(2 * ROWS + ZERO + Y + k, X, stride=ROWS), :] = right_ref[Y_PERT + k]
    for c, b in enumerate((0, 1, 2, 6, 7, 8)):
        for x in range(X):
            new[c, pl.ds((x + 1) * ROWS + ZERO, Y), :] = base_ref[b, pl.ds(x * Y, Y), :]
        new[c, pl.ds(ROWS + ZERO - 1, X, stride=ROWS), :] = left_ref[Y_BASE + c]
        new[c, pl.ds(ROWS + ZERO + Y, X, stride=ROWS), :] = right_ref[Y_BASE + c]
    odd = index_x % 2 == 1
    for ref, high in ((xa_ref, jnp.logical_not(odd)), (xb_ref, odd)):
        for d in (1, 2, 3):
            x = jnp.where(high, X - 1 + d, -d)
            rows = Y + 2 * (3 - d)
            for c in range(9):
                wide[c, pl.ds((x + 3) * ROWS + ZERO - (3 - d), rows), :] = ref[
                    pl.ds(now_row(c, d), rows), :
                ]
            if d < 3:
                pert[pl.ds((x + 2) * ROWS + ZERO - (2 - d), rows - 2), :] = ref[
                    pl.ds(pert_row(d), rows - 2), :
                ]
            if d == 1:
                for c in range(6):
                    new[c, pl.ds((x + 1) * ROWS + ZERO, Y), :] = ref[pl.ds(X_BASE + c * Y, Y), :]

    def row_mask(first, rows):
        y = lax.broadcasted_iota(jnp.int32, (rows, Z), 0) + first
        return ((y >= 0) | (index_y > 0)) & ((y < Y) | (index_y < last_y))

    def plane_valid(x):
        return ((x >= 0) | (index_x > 0)) & ((x < X) | (index_x < last_x))

    def along_z(value):
        lane = lax.broadcasted_iota(jnp.int32, value.shape, 1)
        after = jnp.where(lane < Z - 1, pltpu.roll(value, Z - 1, 1), 0.0)
        before = jnp.where(lane > 0, pltpu.roll(value, 1, 1), 0.0)
        return after - before

    def differences(ref, c, row, rows):
        return (
            ref[c, pl.ds(row + ROWS, rows), :] - ref[c, pl.ds(row - ROWS, rows), :],
            ref[c, pl.ds(row + 1, rows), :] - ref[c, pl.ds(row - 1, rows), :],
            along_z(ref[c, pl.ds(row, rows), :]),
        )

    wide_mask = row_mask(-2, 24)
    lame_rows = jnp.where(wide_mask, 0.5 * lame_ref[...].reshape(1, Z), 0.0)
    shear_rows = jnp.where(wide_mask, shear_ref[...].reshape(1, Z), 0.0)

    @pl.loop(-2, X + 2)
    def _(x):
        row = (x + 3) * ROWS + ZERO - 2
        out = (x + 2) * ROWS + ZERO - 2
        valid = plane_valid(x)
        lame = jnp.where(valid, lame_rows, 0.0)
        shear = jnp.where(valid, shear_rows, 0.0)
        half_shear = 0.5 * shear
        moved = pert[pl.ds(out, 24), :]
        half_moved = 0.5 * moved
        first = None
        for field in range(3):
            gx, gy, gz = zip(*[differences(wide, 3 * field + i, row, 24) for i in range(3)])
            normal = (gx[0], gy[1], gz[2])
            skew = (gy[0] + gx[1], gz[0] + gx[2], gz[1] + gy[2])
            if field == 0:
                first = (normal, skew)
            volume = lame * (gx[0] + gy[1] + gz[2])
            for i in range(3):
                total = shear * normal[i] + volume
                if field == 1:
                    total = total + moved * first[0][i]
                stress[6 * field + i, pl.ds(out, 24), :] = total
                total = half_shear * skew[i]
                if field == 1:
                    total = total + half_moved * first[1][i]
                stress[6 * field + 3 + i, pl.ds(out, 24), :] = total

    new_mask = row_mask(-1, 24)
    scale_rows = jnp.where(new_mask, 0.05 * buoy_ref[...].reshape(1, Z), 0.0)
    top = lax.broadcasted_iota(jnp.int32, (24, Z), 1) == 0
    received_rows = jnp.where(top, 0.1 * buoy_ref[...].reshape(1, Z), 0.0)

    @pl.loop(-1, X + 1)
    def _(x):
        row = (x + 2) * ROWS + ZERO - 1
        out = (x + 1) * ROWS + ZERO - 1
        scale = jnp.where(plane_valid(x), scale_rows, 0.0)

        def across_x(c):
            return stress[c, pl.ds(row + ROWS, 24), :] - stress[c, pl.ds(row - ROWS, 24), :]

        def across_y(c):
            return stress[c, pl.ds(row + 1, 24), :] - stress[c, pl.ds(row - 1, 24), :]

        def across_z(c):
            return along_z(stress[c, pl.ds(row, 24), :])

        change = []
        for field in range(3):
            o = 6 * field
            change.append(
                (
                    scale * (across_x(o) + across_y(o + 3) + across_z(o + 4)),
                    scale * (across_x(o + 3) + across_y(o + 1) + across_z(o + 5)),
                    scale * (across_x(o + 4) + across_y(o + 5) + across_z(o + 2)),
                )
            )
        for i in range(3):
            new[i, pl.ds(out, 24), :] = new[i, pl.ds(out, 24), :] + change[0][i]
            new[3 + i, pl.ds(out, 24), :] = new[3 + i, pl.ds(out, 24), :] + (
                change[2][i] + received_rows * change[1][i]
            )

        @pl.when((x >= 0) & (x < X))
        def _():
            at = pl.multiple_of(x * Y, Y)
            for i in range(3):
                bnext_ref[i, pl.ds(at, Y), :] = (
                    base_ref[3 + i, pl.ds(at, Y), :] + change[1][i][1 : Y + 1]
                )

    @pl.loop(0, X)
    def _(x):
        row = pl.multiple_of((x + 1) * ROWS + ZERO, 8)
        at = pl.multiple_of(x * Y, Y)
        for i in range(3):
            fnext_ref[i, pl.ds(at, Y), :] = new[i, pl.ds(row, Y), :]
            aprev_ref[i, pl.ds(at, Y), :] = new[3 + i, pl.ds(row, Y), :]
        hx, hy, hz = zip(*[differences(new, i, row, Y) for i in range(3)])
        kx, ky, kz = zip(*[differences(new, 3 + i, row, Y) for i in range(3)])
        normal = hx[0] * kx[0] + hy[1] * ky[1] + hz[2] * kz[2]
        skew = (
            (hy[0] + hx[1]) * (ky[0] + kx[1])
            + (hz[0] + hx[2]) * (kz[0] + kx[2])
            + (hz[1] + hy[2]) * (kz[1] + ky[2])
        )
        hess_ref[pl.ds(at, Y), :] = -0.0125 * (2.0 * normal + skew)


def shape(*dims):
    return jax.ShapeDtypeStruct(dims, F32)


HBM = pl.BlockSpec(memory_space=pltpu.HBM)
VMEM = pl.BlockSpec(memory_space=pltpu.VMEM)
SMEM = pl.BlockSpec(memory_space=pltpu.SMEM)


def on_device(
    forward_prev,
    forward_now,
    born_prev,
    born_now,
    adjoint_now,
    adjoint_next,
    shear_pert,
    lame_depth,
    shear_depth,
    buoyancy,
    drm_cells,
    drm_matrix,
    drm_motion,
    source_cell,
    source_force,
):
    assert forward_now.shape == (1, 3, X, Y, Z)
    count_x = lax.axis_size("gx")
    count_y = lax.axis_size("gy")
    events = lax.axis_size("event")
    place = jnp.stack(
        [
            lax.axis_index("gx"),
            lax.axis_index("gy"),
            jnp.int32(count_y * Y),
            jnp.int32(count_x),
            jnp.int32(count_y),
        ]
    ).astype(jnp.int32)
    flat = [
        a.reshape(3, CELLS, Z)
        for a in (forward_prev, forward_now, born_prev, born_now, adjoint_now, adjoint_next)
    ]
    pert = shear_pert.reshape(CELLS, Z)
    lame, shear, buoy = (a.reshape(1, Z) for a in (lame_depth, shear_depth, buoyancy))

    begin_inputs = (
        *flat,
        pert,
        buoy,
        drm_cells.reshape(1, ELEMS),
        drm_matrix.reshape(9, 1, ELEMS),
        drm_motion.reshape(3, 1, ELEMS),
        source_cell,
        source_force,
    )
    base, low, high, xa, xb = pl.pallas_call(
        begin_kernel,
        out_shape=(
            shape(9, CELLS, Z),
            shape(Y_PLANES, X, Z),
            shape(Y_PLANES, X, Z),
            shape(X_ROWS, Z),
            shape(X_ROWS, Z),
        ),
        in_specs=[SMEM] + [HBM] * 13,
        out_specs=[VMEM] * 5,
        scratch_shapes=[pltpu.VMEM((3, CELLS, Z), F32)]
        + [pltpu.VMEM(a.shape, a.dtype) for a in begin_inputs[:11]]
        + [pltpu.SMEM((1,), jnp.int32), pltpu.VMEM((1, 3), F32)]
        + [pltpu.SemaphoreType.DMA((13,))],
        compiler_params=pltpu.CompilerParams(vmem_limit_bytes=60 * 2**20),
        name="begin",
    )(
        place,
        *begin_inputs,
    )

    left = lax.ppermute(high, "gy", [(i, i + 1) for i in range(count_y - 1)])
    right = lax.ppermute(low, "gy", [(i + 1, i) for i in range(count_y - 1)])

    xa, xb = pl.pallas_call(
        widen_kernel,
        out_shape=(shape(X_ROWS, Z), shape(X_ROWS, Z)),
        in_specs=[SMEM] + [VMEM] * 4,
        out_specs=[VMEM] * 2,
        compiler_params=pltpu.CompilerParams(vmem_limit_bytes=16 * 2**20),
        name="widen",
    )(place, xa, xb, left, right)

    def swap(first):
        pairs = []
        for i in range(first, count_x - 1, 2):
            pairs += [(i, i + 1), (i + 1, i)]
        return pairs

    xa = lax.ppermute(xa, "gx", swap(0))
    xb = lax.ppermute(xb, "gx", swap(1))

    hess, forward_next, born_next, adjoint_prev = pl.pallas_call(
        step_kernel,
        out_shape=(shape(CELLS, Z), shape(3, CELLS, Z), shape(3, CELLS, Z), shape(3, CELLS, Z)),
        in_specs=[SMEM] + [VMEM] * 12,
        out_specs=[VMEM] * 4,
        scratch_shapes=[
            pltpu.VMEM((9, (X + 6) * ROWS, Z), F32),
            pltpu.VMEM(((X + 4) * ROWS, Z), F32),
            pltpu.VMEM((18, (X + 4) * ROWS, Z), F32),
            pltpu.VMEM((6, (X + 2) * ROWS, Z), F32),
        ],
        compiler_params=pltpu.CompilerParams(vmem_limit_bytes=36 * 2**20),
        name="step",
    )(
        place,
        flat[1],
        flat[3],
        flat[4],
        pert,
        base,
        left,
        right,
        xa,
        xb,
        lame,
        shear,
        buoy,
    )

    parts = lax.all_to_all(hess.reshape(events, CELLS // events, Z), "event", 0, 0, tiled=True)
    part = jnp.sum(parts, axis=0)
    spread = jnp.broadcast_to(part[None], (events, CELLS // events, Z))
    hess = lax.all_to_all(spread, "event", 0, 0, tiled=True)

    whole = (1, 3, X, Y, Z)
    return (
        hess.reshape(X, Y, Z),
        forward_next.reshape(whole),
        born_next.reshape(whole),
        adjoint_prev.reshape(whole),
    )


def solution(mesh):
    field = P("event", None, "gx", "gy", None)
    return jax.shard_map(
        on_device,
        mesh=mesh,
        in_specs=(field,) * 6
        + (
            P("gx", "gy", None),
            P(),
            P(),
            P(),
            P("gx", "gy", None),
            P(None, None, "gx", "gy", None),
            P("event", None, "gx", "gy", None),
            P("event"),
            P("event", None),
        ),
        out_specs=(P("gx", "gy", None), field, field, field),
        check_vma=False,
    )
```

```python
import functools

import jax
import jax.numpy as jnp
from jax import lax
from jax.experimental import pallas as pl
from jax.experimental.pallas import tpu as pltpu
from jax.sharding import PartitionSpec as P

X = 16
Y = 16
Z = 128
CELLS = X * Y
LAYER = 4
ELEMS = CELLS * LAYER

Y_BASE = 27
Y_PERT = 33
Y_PLANES = 35

X_STEP = 54
X_PERT = 9 * X_STEP
X_BASE = X_PERT + 34
X_ROWS = X_BASE + 6 * Y

ROWS = 32
ZERO = 8

F32 = jnp.float32


def now_row(c, d):
    return c * X_STEP + (0, 20, 38)[d - 1]


def pert_row(d):
    return X_PERT + (0, 18)[d - 1]


def near_x(high, d):
    return jnp.where(high, X - d, d - 1)


def element_force(depth, matrix_ref, motion_ref):
    slot = lax.broadcasted_iota(jnp.int32, (16, ELEMS), 0)
    spread = jnp.zeros((16, ELEMS), F32)
    for i in range(3):
        element = sum(
            matrix_ref[3 * i + c].reshape(1, ELEMS) * motion_ref[c].reshape(1, ELEMS)
            for c in range(3)
        )
        spread = jnp.where(slot == depth - (Z - 16) - 4 * i, element, spread)
    rest = jnp.concatenate([jnp.zeros((Z - 16, ELEMS), F32), spread], axis=0)
    parts = []
    for _ in range(3):
        parts.append(rest.astype(jnp.bfloat16))
        rest = rest - parts[-1].astype(F32)
    return parts


def placed_force(columns, cells_ref, matrix_ref, motion_ref):
    rows = columns.shape[0]
    cells = cells_ref[...].reshape(1, ELEMS)
    pick = jnp.where(columns == cells // Z, 1.0, 0.0).astype(jnp.bfloat16)
    placed = jnp.zeros((rows, Z), F32)
    for part in element_force(cells % Z, matrix_ref, motion_ref):
        placed = placed + lax.dot_general(
            pick, part, (((1,), (1,)), ((), ())), preferred_element_type=F32
        )
    lane = lax.broadcasted_iota(jnp.int32, (rows, Z), 1)
    applied = []
    for i in range(3):
        moved = placed if i == 0 else pltpu.roll(placed, 4 * i, 1)
        applied.append(jnp.where(lane >= Z - LAYER, moved, 0.0))
    return applied


def plane_rows(ref, y):
    return ref[pl.ds(y, X, stride=Y), :]


def begin_kernel(*refs):
    sources, low_ref, high_ref = refs[:11], refs[11], refs[12]
    held, arrived = refs[13:24], refs[24]
    copies = [
        pltpu.make_async_copy(source, ref, arrived.at[i])
        for i, (source, ref) in enumerate(zip(sources, held))
    ]
    order = (8, 9, 10, 1, 3, 4, 6, 7, 0, 2, 5)
    for i in order:
        copies[i].start()
    fprev_ref, fnow_ref, bprev_ref, bnow_ref, anow_ref, anext_ref = held[:6]
    pert_ref, buoy_ref, cells_ref, matrix_ref, motion_ref = held[6:]
    for i in order[:3]:
        copies[i].wait()

    row = lax.broadcasted_iota(jnp.int32, (2 * X, ELEMS), 0)
    columns = (row % X) * Y + jnp.where(row < X, 0, Y - 1)
    applied = placed_force(columns, cells_ref, matrix_ref, motion_ref)

    for i in order[3:7]:
        copies[i].wait()
    now = [r.at[i] for r in (fnow_ref, bnow_ref, anow_ref) for i in range(3)]
    for c in range(9):
        for k in range(3):
            low_ref[3 * c + k] = plane_rows(now[c], k)
            high_ref[3 * c + k] = plane_rows(now[c], Y - 3 + k)
    for k in range(2):
        low_ref[Y_PERT + k] = plane_rows(pert_ref, k)
        high_ref[Y_PERT + k] = plane_rows(pert_ref, Y - 2 + k)

    for i in order[7:]:
        copies[i].wait()
    scale = 0.1 * buoy_ref[...].reshape(1, Z)
    top = lax.broadcasted_iota(jnp.int32, (1, Z), 1) == 0
    surface_scale = jnp.where(top, scale, 0.0)
    for ref, y, first in ((low_ref, 0, 0), (high_ref, Y - 1, X)):
        for i in range(3):
            ref[Y_BASE + i] = (
                2.0 * plane_rows(now[i], y)
                - plane_rows(fprev_ref.at[i], y)
                + scale * applied[i][first : first + X]
            )
            born = 2.0 * plane_rows(now[3 + i], y) - plane_rows(bprev_ref.at[i], y)
            ref[Y_BASE + 3 + i] = (
                2.0 * plane_rows(now[6 + i], y)
                - plane_rows(anext_ref.at[i], y)
                + surface_scale * born
            )


def base_kernel(
    fprev_ref,
    fnow_ref,
    bprev_ref,
    bnow_ref,
    anow_ref,
    anext_ref,
    pert_ref,
    buoy_ref,
    cells_ref,
    matrix_ref,
    motion_ref,
    base_ref,
    xa_ref,
    xb_ref,
):
    columns = lax.broadcasted_iota(jnp.int32, (CELLS, ELEMS), 0)
    applied = placed_force(columns, cells_ref, matrix_ref, motion_ref)
    scale = 0.1 * buoy_ref[...].reshape(1, Z)
    top = lax.broadcasted_iota(jnp.int32, (1, Z), 1) == 0
    surface_scale = jnp.where(top, scale, 0.0)
    for i in range(3):
        base_ref[i] = 2.0 * fnow_ref[i] - fprev_ref[i] + scale * applied[i]
        born = 2.0 * bnow_ref[i] - bprev_ref[i]
        base_ref[3 + i] = born
        base_ref[6 + i] = 2.0 * anow_ref[i] - anext_ref[i] + surface_scale * born

    now = [r.at[i] for r in (fnow_ref, bnow_ref, anow_ref) for i in range(3)]
    bases = [base_ref.at[i] for i in (0, 1, 2, 6, 7, 8)]
    odd = lax.axis_index("gx") % 2 == 1
    for ref, high in ((xa_ref, jnp.logical_not(odd)), (xb_ref, odd)):

        def plane_of(source, d):
            start = pl.multiple_of(near_x(high, d) * Y, Y)
            return source[pl.ds(start, Y), :]

        for c in range(9):
            for d in (1, 2, 3):
                ref[pl.ds(now_row(c, d) + 3 - d, Y), :] = plane_of(now[c], d)
        for d in (1, 2):
            ref[pl.ds(pert_row(d) + 2 - d, Y), :] = plane_of(pert_ref, d)
        for c in range(6):
            ref[pl.ds(X_BASE + c * Y, Y), :] = plane_of(bases[c], 1)


def widen_kernel(xa_in, xb_in, left_ref, right_ref, xa_ref, xb_ref):
    odd = lax.axis_index("gx") % 2 == 1
    for source, ref, high in ((xa_in, xa_ref, jnp.logical_not(odd)), (xb_in, xb_ref, odd)):
        ref[...] = source[...]
        for d in (1, 2):
            x = near_x(high, d)
            for c in range(9):
                start = now_row(c, d)
                for k in range(3 - d):
                    ref[pl.ds(start + k, 1), :] = left_ref[3 * c + d + k, pl.ds(x, 1), :]
                    ref[pl.ds(start + 19 - d + k, 1), :] = right_ref[3 * c + k, pl.ds(x, 1), :]
        x = near_x(high, 1)
        ref[pl.ds(pert_row(1), 1), :] = left_ref[Y_PERT + 1, pl.ds(x, 1), :]
        ref[pl.ds(pert_row(1) + 17, 1), :] = right_ref[Y_PERT, pl.ds(x, 1), :]


def step_kernel(
    count_x,
    count_y,
    fnow_ref,
    bnow_ref,
    anow_ref,
    pert_in,
    base_ref,
    left_ref,
    right_ref,
    xa_ref,
    xb_ref,
    lame_ref,
    shear_ref,
    buoy_ref,
    cell_ref,
    force_ref,
    hess_ref,
    fnext_ref,
    bnext_ref,
    aprev_ref,
    wide,
    pert,
    stress,
    new,
):
    index_x, index_y = lax.axis_index("gx"), lax.axis_index("gy")
    last_x, last_y = count_x - 1, count_y - 1

    now = [r.at[i] for r in (fnow_ref, bnow_ref, anow_ref) for i in range(3)]
    for c in range(9):
        for x in range(X):
            wide[c, pl.ds((x + 3) * ROWS + ZERO, Y), :] = now[c][pl.ds(x * Y, Y), :]
        for k in range(3):
            wide[c, pl.ds(3 * ROWS + ZERO - 3 + k, X, stride=ROWS), :] = left_ref[3 * c + k]
            wide[c, pl.ds(3 * ROWS + ZERO + Y + k, X, stride=ROWS), :] = right_ref[3 * c + k]
    for x in range(X):
        pert[pl.ds((x + 2) * ROWS + ZERO, Y), :] = pert_in[pl.ds(x * Y, Y), :]
    for k in range(2):
        pert[pl.ds(2 * ROWS + ZERO - 2 + k, X, stride=ROWS), :] = left_ref[Y_PERT + k]
        pert[pl.ds(2 * ROWS + ZERO + Y + k, X, stride=ROWS), :] = right_ref[Y_PERT + k]
    for c, b in enumerate((0, 1, 2, 6, 7, 8)):
        for x in range(X):
            new[c, pl.ds((x + 1) * ROWS + ZERO, Y), :] = base_ref[b, pl.ds(x * Y, Y), :]
        new[c, pl.ds(ROWS + ZERO - 1, X, stride=ROWS), :] = left_ref[Y_BASE + c]
        new[c, pl.ds(ROWS + ZERO + Y, X, stride=ROWS), :] = right_ref[Y_BASE + c]
    odd = index_x % 2 == 1
    for ref, high in ((xa_ref, jnp.logical_not(odd)), (xb_ref, odd)):
        for d in (1, 2, 3):
            x = jnp.where(high, X - 1 + d, -d)
            rows = Y + 2 * (3 - d)
            for c in range(9):
                wide[c, pl.ds((x + 3) * ROWS + ZERO - (3 - d), rows), :] = ref[
                    pl.ds(now_row(c, d), rows), :
                ]
            if d < 3:
                pert[pl.ds((x + 2) * ROWS + ZERO - (2 - d), rows - 2), :] = ref[
                    pl.ds(pert_row(d), rows - 2), :
                ]
            if d == 1:
                for c in range(6):
                    new[c, pl.ds((x + 1) * ROWS + ZERO, Y), :] = ref[pl.ds(X_BASE + c * Y, Y), :]

    def row_mask(first, rows):
        y = lax.broadcasted_iota(jnp.int32, (rows, Z), 0) + first
        return ((y >= 0) | (index_y > 0)) & ((y < Y) | (index_y < last_y))

    def plane_valid(x):
        return ((x >= 0) | (index_x > 0)) & ((x < X) | (index_x < last_x))

    def along_z(value):
        lane = lax.broadcasted_iota(jnp.int32, value.shape, 1)
        after = jnp.where(lane < Z - 1, pltpu.roll(value, Z - 1, 1), 0.0)
        before = jnp.where(lane > 0, pltpu.roll(value, 1, 1), 0.0)
        return after - before

    def differences(ref, c, row, rows):
        return (
            ref[c, pl.ds(row + ROWS, rows), :] - ref[c, pl.ds(row - ROWS, rows), :],
            ref[c, pl.ds(row + 1, rows), :] - ref[c, pl.ds(row - 1, rows), :],
            along_z(ref[c, pl.ds(row, rows), :]),
        )

    wide_mask = row_mask(-2, 24)
    lame_rows = jnp.where(wide_mask, 0.5 * lame_ref[...].reshape(1, Z), 0.0)
    shear_rows = jnp.where(wide_mask, shear_ref[...].reshape(1, Z), 0.0)

    @pl.loop(-2, X + 2, unroll=X + 4)
    def _(x):
        row = (x + 3) * ROWS + ZERO - 2
        out = (x + 2) * ROWS + ZERO - 2
        valid = plane_valid(x)
        lame = jnp.where(valid, lame_rows, 0.0)
        shear = jnp.where(valid, shear_rows, 0.0)
        half_shear = 0.5 * shear
        moved = pert[pl.ds(out, 24), :]
        half_moved = 0.5 * moved
        first = None
        for field in range(3):
            gx, gy, gz = zip(*[differences(wide, 3 * field + i, row, 24) for i in range(3)])
            normal = (gx[0], gy[1], gz[2])
            skew = (gy[0] + gx[1], gz[0] + gx[2], gz[1] + gy[2])
            if field == 0:
                first = (normal, skew)
            volume = lame * (gx[0] + gy[1] + gz[2])
            for i in range(3):
                total = shear * normal[i] + volume
                if field == 1:
                    total = total + moved * first[0][i]
                stress[6 * field + i, pl.ds(out, 24), :] = total
                total = half_shear * skew[i]
                if field == 1:
                    total = total + half_moved * first[1][i]
                stress[6 * field + 3 + i, pl.ds(out, 24), :] = total

    new_mask = row_mask(-1, 24)
    scale_rows = jnp.where(new_mask, 0.05 * buoy_ref[...].reshape(1, Z), 0.0)
    top = lax.broadcasted_iota(jnp.int32, (24, Z), 1) == 0
    point_rows = jnp.where(new_mask, 0.1 * buoy_ref[...].reshape(1, Z), 0.0)
    received_rows = jnp.where(top, point_rows, 0.0)
    point = [point_rows * force_ref[:, i : i + 1] for i in range(3)]
    first_cell = (index_y * Y - 1 + lax.broadcasted_iota(jnp.int32, (24, Z), 0)) * Z
    source_row = cell_ref[...] - first_cell

    @pl.loop(-1, X + 1, unroll=X + 2)
    def _(x):
        row = (x + 2) * ROWS + ZERO - 1
        out = (x + 1) * ROWS + ZERO - 1
        scale = jnp.where(plane_valid(x), scale_rows, 0.0)

        def across_x(c):
            return stress[c, pl.ds(row + ROWS, 24), :] - stress[c, pl.ds(row - ROWS, 24), :]

        def across_y(c):
            return stress[c, pl.ds(row + 1, 24), :] - stress[c, pl.ds(row - 1, 24), :]

        def across_z(c):
            return along_z(stress[c, pl.ds(row, 24), :])

        change = []
        for field in range(3):
            o = 6 * field
            change.append(
                (
                    scale * (across_x(o) + across_y(o + 3) + across_z(o + 4)),
                    scale * (across_x(o + 3) + across_y(o + 1) + across_z(o + 5)),
                    scale * (across_x(o + 4) + across_y(o + 5) + across_z(o + 2)),
                )
            )
        here = source_row == (index_x * X + x) * (count_y * Y * Z)
        for i in range(3):
            new[i, pl.ds(out, 24), :] = new[i, pl.ds(out, 24), :] + (
                change[0][i] + jnp.where(here, point[i], 0.0)
            )
            new[3 + i, pl.ds(out, 24), :] = new[3 + i, pl.ds(out, 24), :] + (
                change[2][i] + received_rows * change[1][i]
            )

        @pl.when((x >= 0) & (x < X))
        def _():
            at = pl.multiple_of(x * Y, Y)
            for i in range(3):
                bnext_ref[i, pl.ds(at, Y), :] = (
                    base_ref[3 + i, pl.ds(at, Y), :] + change[1][i][1 : Y + 1]
                )

    @pl.loop(0, X, unroll=X)
    def _(x):
        row = pl.multiple_of((x + 1) * ROWS + ZERO, 8)
        at = pl.multiple_of(x * Y, Y)
        for i in range(3):
            fnext_ref[i, pl.ds(at, Y), :] = new[i, pl.ds(row, Y), :]
            aprev_ref[i, pl.ds(at, Y), :] = new[3 + i, pl.ds(row, Y), :]
        hx, hy, hz = zip(*[differences(new, i, row, Y) for i in range(3)])
        kx, ky, kz = zip(*[differences(new, 3 + i, row, Y) for i in range(3)])
        normal = hx[0] * kx[0] + hy[1] * ky[1] + hz[2] * kz[2]
        skew = (
            (hy[0] + hx[1]) * (ky[0] + kx[1])
            + (hz[0] + hx[2]) * (kz[0] + kx[2])
            + (hz[1] + hy[2]) * (kz[1] + ky[2])
        )
        hess_ref[pl.ds(at, Y), :] = -0.0125 * (2.0 * normal + skew)


def shape(*dims):
    return jax.ShapeDtypeStruct(dims, F32)


HBM = pl.BlockSpec(memory_space=pltpu.HBM)
VMEM = pl.BlockSpec(memory_space=pltpu.VMEM)


def on_device(
    forward_prev,
    forward_now,
    born_prev,
    born_now,
    adjoint_now,
    adjoint_next,
    shear_pert,
    lame_depth,
    shear_depth,
    buoyancy,
    drm_cells,
    drm_matrix,
    drm_motion,
    source_cell,
    source_force,
):
    assert forward_now.shape == (1, 3, X, Y, Z)
    count_x = lax.axis_size("gx")
    count_y = lax.axis_size("gy")
    events = lax.axis_size("event")
    flat = [
        a.reshape(3, CELLS, Z)
        for a in (forward_prev, forward_now, born_prev, born_now, adjoint_now, adjoint_next)
    ]
    pert = shear_pert.reshape(CELLS, Z)
    lame, shear, buoy = (a.reshape(1, Z) for a in (lame_depth, shear_depth, buoyancy))

    begin_inputs = (
        *flat,
        pert,
        buoy,
        drm_cells.reshape(1, ELEMS),
        drm_matrix.reshape(9, 1, ELEMS),
        drm_motion.reshape(3, 1, ELEMS),
    )
    low, high = pl.pallas_call(
        begin_kernel,
        out_shape=(shape(Y_PLANES, X, Z), shape(Y_PLANES, X, Z)),
        in_specs=[HBM] * 11,
        out_specs=[VMEM] * 2,
        scratch_shapes=[pltpu.VMEM(a.shape, a.dtype) for a in begin_inputs]
        + [pltpu.SemaphoreType.DMA((11,))],
        compiler_params=pltpu.CompilerParams(vmem_limit_bytes=60 * 2**20),
        name="begin",
    )(*begin_inputs)

    left = lax.ppermute(high, "gy", [(i, i + 1) for i in range(count_y - 1)])
    right = lax.ppermute(low, "gy", [(i + 1, i) for i in range(count_y - 1)])

    base, xa, xb = pl.pallas_call(
        base_kernel,
        out_shape=(shape(9, CELLS, Z), shape(X_ROWS, Z), shape(X_ROWS, Z)),
        in_specs=[VMEM] * 11,
        out_specs=[VMEM] * 3,
        compiler_params=pltpu.CompilerParams(vmem_limit_bytes=16 * 2**20),
        name="base",
    )(*begin_inputs)

    xa, xb = pl.pallas_call(
        widen_kernel,
        out_shape=(shape(X_ROWS, Z), shape(X_ROWS, Z)),
        in_specs=[VMEM] * 4,
        out_specs=[VMEM] * 2,
        compiler_params=pltpu.CompilerParams(vmem_limit_bytes=4 * 2**20),
        name="widen",
    )(xa, xb, left, right)

    def swap(first):
        pairs = []
        for i in range(first, count_x - 1, 2):
            pairs += [(i, i + 1), (i + 1, i)]
        return pairs

    xa = lax.ppermute(xa, "gx", swap(0))
    xb = lax.ppermute(xb, "gx", swap(1))

    hess, forward_next, born_next, adjoint_prev = pl.pallas_call(
        functools.partial(step_kernel, count_x, count_y),
        out_shape=(shape(CELLS, Z), shape(3, CELLS, Z), shape(3, CELLS, Z), shape(3, CELLS, Z)),
        in_specs=[VMEM] * 14,
        out_specs=[VMEM] * 4,
        scratch_shapes=[
            pltpu.VMEM((9, (X + 6) * ROWS, Z), F32),
            pltpu.VMEM(((X + 4) * ROWS, Z), F32),
            pltpu.VMEM((18, (X + 4) * ROWS, Z), F32),
            pltpu.VMEM((6, (X + 2) * ROWS, Z), F32),
        ],
        compiler_params=pltpu.CompilerParams(vmem_limit_bytes=20 * 2**20),
        name="step",
    )(
        flat[1],
        flat[3],
        flat[4],
        pert,
        base,
        left,
        right,
        xa,
        xb,
        lame,
        shear,
        buoy,
        source_cell[:, None] - lax.broadcasted_iota(jnp.int32, (1, Z), 1),
        source_force,
    )

    parts = lax.all_to_all(hess.reshape(events, CELLS // events, Z), "event", 0, 0, tiled=True)
    part = jnp.sum(parts, axis=0)
    spread = jnp.broadcast_to(part[None], (events, CELLS // events, Z))
    hess = lax.all_to_all(spread, "event", 0, 0, tiled=True)

    whole = (1, 3, X, Y, Z)
    return (
        hess.reshape(X, Y, Z),
        forward_next.reshape(whole),
        born_next.reshape(whole),
        adjoint_prev.reshape(whole),
    )


def solution(mesh):
    field = P("event", None, "gx", "gy", None)
    return jax.shard_map(
        on_device,
        mesh=mesh,
        in_specs=(field,) * 6
        + (
            P("gx", "gy", None),
            P(),
            P(),
            P(),
            P("gx", "gy", None),
            P(None, None, "gx", "gy", None),
            P("event", None, "gx", "gy", None),
            P("event"),
            P("event", None),
        ),
        out_specs=(P("gx", "gy", None), field, field, field),
        check_vma=False,
    )
```

```python
import functools

import jax
import jax.numpy as jnp
from jax import lax
from jax.experimental import pallas as pl
from jax.experimental.pallas import tpu as pltpu
from jax.sharding import PartitionSpec as P

X = 16
Y = 16
Z = 128
CELLS = X * Y
LAYER = 4
ELEMS = CELLS * LAYER

Y_BASE = 18
Y_PERT = 24
Y_PLANES = 26

X_STEP = 38
X_PERT = 9 * X_STEP
X_BASE = X_PERT + 34
X_ROWS = X_BASE + 6 * Y

ROWS = 32
ZERO = 8

F32 = jnp.float32


def now_row(c, d):
    return c * X_STEP + (0, 20)[d - 1]


def pert_row(d):
    return X_PERT + (0, 18)[d - 1]


def near_x(high, d):
    return jnp.where(high, X - d, d - 1)


def element_force(depth, matrix_ref, motion_ref):
    slot = lax.broadcasted_iota(jnp.int32, (16, ELEMS), 0)
    spread = jnp.zeros((16, ELEMS), F32)
    for i in range(3):
        element = sum(
            matrix_ref[3 * i + c].reshape(1, ELEMS) * motion_ref[c].reshape(1, ELEMS)
            for c in range(3)
        )
        spread = jnp.where(slot == depth - (Z - 16) - 4 * i, element, spread)
    rest = jnp.concatenate([jnp.zeros((Z - 16, ELEMS), F32), spread], axis=0)
    parts = []
    for _ in range(3):
        parts.append(rest.astype(jnp.bfloat16))
        rest = rest - parts[-1].astype(F32)
    return parts


def placed_force(columns, cells_ref, matrix_ref, motion_ref):
    rows = columns.shape[0]
    cells = cells_ref[...].reshape(1, ELEMS)
    pick = jnp.where(columns == cells // Z, 1.0, 0.0).astype(jnp.bfloat16)
    placed = jnp.zeros((rows, Z), F32)
    for part in element_force(cells % Z, matrix_ref, motion_ref):
        placed = placed + lax.dot_general(
            pick, part, (((1,), (1,)), ((), ())), preferred_element_type=F32
        )
    lane = lax.broadcasted_iota(jnp.int32, (rows, Z), 1)
    applied = []
    for i in range(3):
        moved = placed if i == 0 else pltpu.roll(placed, 4 * i, 1)
        applied.append(jnp.where(lane >= Z - LAYER, moved, 0.0))
    return applied


def edge_coefficients(shear, lame, along):
    return [2.0 * shear + lame if i == along else shear for i in range(3)]


def edge_bases(lame_ref, shear_ref, buoy_ref, along, bases, far, pert):
    scale = 0.1 * buoy_ref[...].reshape(1, Z)
    top = lax.broadcasted_iota(jnp.int32, (1, Z), 1) == 0
    surface_scale = jnp.where(top, scale, 0.0)
    quarter = 0.25 * scale
    coefficients = edge_coefficients(
        quarter * shear_ref[...].reshape(1, Z), quarter * lame_ref[...].reshape(1, Z), along
    )
    forward, adjoint = [], []
    for i in range(3):
        moved = quarter * pert * (2.0 if i == along else 1.0)
        forward.append(bases[0][i] + coefficients[i] * far[0][i])
        born = bases[1][i] + coefficients[i] * far[1][i] + moved * far[0][i]
        adjoint.append(bases[2][i] + coefficients[i] * far[2][i] + surface_scale * born)
    return forward + adjoint


def plane_rows(ref, y):
    return ref[pl.ds(y, X, stride=Y), :]


def begin_kernel(*refs):
    sources, low_ref, high_ref = refs[:13], refs[13], refs[14]
    held, arrived = refs[15:28], refs[28]
    copies = [
        pltpu.make_async_copy(source, ref, arrived.at[i])
        for i, (source, ref) in enumerate(zip(sources, held))
    ]
    order = (8, 9, 10, 1, 3, 4, 6, 7, 11, 12, 0, 2, 5)
    for i in order:
        copies[i].start()
    fprev_ref, fnow_ref, bprev_ref, bnow_ref, anow_ref, anext_ref = held[:6]
    pert_ref, buoy_ref, cells_ref, matrix_ref, motion_ref, lame_ref, shear_ref = held[6:]
    for i in order[:3]:
        copies[i].wait()

    row = lax.broadcasted_iota(jnp.int32, (2 * X, ELEMS), 0)
    columns = (row % X) * Y + jnp.where(row < X, 0, Y - 1)
    applied = placed_force(columns, cells_ref, matrix_ref, motion_ref)

    for i in order[3:9]:
        copies[i].wait()
    now = [r.at[i] for r in (fnow_ref, bnow_ref, anow_ref) for i in range(3)]
    for c in range(9):
        for k in range(2):
            low_ref[2 * c + k] = plane_rows(now[c], k)
            high_ref[2 * c + k] = plane_rows(now[c], Y - 2 + k)
    for k in range(2):
        low_ref[Y_PERT + k] = plane_rows(pert_ref, k)
        high_ref[Y_PERT + k] = plane_rows(pert_ref, Y - 2 + k)

    for i in order[9:]:
        copies[i].wait()
    scale = 0.1 * buoy_ref[...].reshape(1, Z)
    for ref, y, step, first in ((low_ref, 0, 1, 0), (high_ref, Y - 1, -1, X)):
        bases = [
            [2.0 * plane_rows(now[3 * f + i], y) - plane_rows(old.at[i], y) for i in range(3)]
            for f, old in enumerate((fprev_ref, bprev_ref, anext_ref))
        ]
        for i in range(3):
            bases[0][i] = bases[0][i] + scale * applied[i][first : first + X]
        far = [[plane_rows(now[3 * f + i], y + 2 * step) for i in range(3)] for f in range(3)]
        sent = edge_bases(
            lame_ref, shear_ref, buoy_ref, 1, bases, far, plane_rows(pert_ref, y + step)
        )
        for c in range(6):
            ref[Y_BASE + c] = sent[c]


def base_kernel(
    fprev_ref,
    fnow_ref,
    bprev_ref,
    bnow_ref,
    anow_ref,
    anext_ref,
    pert_ref,
    buoy_ref,
    cells_ref,
    matrix_ref,
    motion_ref,
    lame_ref,
    shear_ref,
    base_ref,
    xa_ref,
    xb_ref,
):
    columns = lax.broadcasted_iota(jnp.int32, (CELLS, ELEMS), 0)
    applied = placed_force(columns, cells_ref, matrix_ref, motion_ref)
    scale = 0.1 * buoy_ref[...].reshape(1, Z)
    top = lax.broadcasted_iota(jnp.int32, (1, Z), 1) == 0
    surface_scale = jnp.where(top, scale, 0.0)
    for i in range(3):
        base_ref[i] = 2.0 * fnow_ref[i] - fprev_ref[i] + scale * applied[i]
        born = 2.0 * bnow_ref[i] - bprev_ref[i]
        base_ref[3 + i] = born
        base_ref[6 + i] = 2.0 * anow_ref[i] - anext_ref[i] + surface_scale * born

    now = [r.at[i] for r in (fnow_ref, bnow_ref, anow_ref) for i in range(3)]
    odd = lax.axis_index("gx") % 2 == 1
    for ref, high in ((xa_ref, jnp.logical_not(odd)), (xb_ref, odd)):

        def plane_of(source, d):
            start = pl.multiple_of(near_x(high, d) * Y, Y)
            return source[pl.ds(start, Y), :]

        for c in range(9):
            for d in (1, 2):
                ref[pl.ds(now_row(c, d) + 3 - d, Y), :] = plane_of(now[c], d)
        for d in (1, 2):
            ref[pl.ds(pert_row(d) + 2 - d, Y), :] = plane_of(pert_ref, d)
        bases = [[plane_of(base_ref.at[3 * f + i], 1) for i in range(3)] for f in range(3)]
        for i in range(3):
            bases[2][i] = 2.0 * plane_of(now[6 + i], 1) - plane_of(anext_ref.at[i], 1)
        far = [[plane_of(now[3 * f + i], 3) for i in range(3)] for f in range(3)]
        sent = edge_bases(
            lame_ref, shear_ref, buoy_ref, 0, bases, far, plane_of(pert_ref, 2)
        )
        for c in range(6):
            ref[pl.ds(X_BASE + c * Y, Y), :] = sent[c]


def widen_kernel(xa_in, xb_in, left_ref, right_ref, xa_ref, xb_ref):
    odd = lax.axis_index("gx") % 2 == 1
    for source, ref, high in ((xa_in, xa_ref, jnp.logical_not(odd)), (xb_in, xb_ref, odd)):
        ref[...] = source[...]
        for d in (1, 2):
            x = near_x(high, d)
            for c in range(9):
                start = now_row(c, d)
                for k in range(3 - d):
                    ref[pl.ds(start + k, 1), :] = left_ref[2 * c + d - 1 + k, pl.ds(x, 1), :]
                    ref[pl.ds(start + 19 - d + k, 1), :] = right_ref[2 * c + k, pl.ds(x, 1), :]
        x = near_x(high, 1)
        ref[pl.ds(pert_row(1), 1), :] = left_ref[Y_PERT + 1, pl.ds(x, 1), :]
        ref[pl.ds(pert_row(1) + 17, 1), :] = right_ref[Y_PERT, pl.ds(x, 1), :]


def step_kernel(
    count_x,
    count_y,
    fnow_ref,
    bnow_ref,
    anow_ref,
    pert_in,
    base_ref,
    left_ref,
    right_ref,
    xa_ref,
    xb_ref,
    lame_ref,
    shear_ref,
    buoy_ref,
    cell_ref,
    force_ref,
    hess_ref,
    fnext_ref,
    bnext_ref,
    aprev_ref,
    wide,
    pert,
    stress,
    new,
):
    index_x, index_y = lax.axis_index("gx"), lax.axis_index("gy")
    last_x, last_y = count_x - 1, count_y - 1

    now = [r.at[i] for r in (fnow_ref, bnow_ref, anow_ref) for i in range(3)]
    for c in range(9):
        for x in range(X):
            wide[c, pl.ds((x + 3) * ROWS + ZERO, Y), :] = now[c][pl.ds(x * Y, Y), :]
        for k in range(2):
            wide[c, pl.ds(3 * ROWS + ZERO - 2 + k, X, stride=ROWS), :] = left_ref[2 * c + k]
            wide[c, pl.ds(3 * ROWS + ZERO + Y + k, X, stride=ROWS), :] = right_ref[2 * c + k]
        for row in (ZERO - 3, ZERO + Y + 2):
            wide[c, pl.ds(3 * ROWS + row, X, stride=ROWS), :] = jnp.zeros((X, Z), F32)
        for plane in (0, X + 5):
            wide[c, pl.ds(plane * ROWS + ZERO, Y), :] = jnp.zeros((Y, Z), F32)
    for x in range(X):
        pert[pl.ds((x + 2) * ROWS + ZERO, Y), :] = pert_in[pl.ds(x * Y, Y), :]
    for k in range(2):
        pert[pl.ds(2 * ROWS + ZERO - 2 + k, X, stride=ROWS), :] = left_ref[Y_PERT + k]
        pert[pl.ds(2 * ROWS + ZERO + Y + k, X, stride=ROWS), :] = right_ref[Y_PERT + k]
    for c, b in enumerate((0, 1, 2, 6, 7, 8)):
        for x in range(X):
            new[c, pl.ds((x + 1) * ROWS + ZERO, Y), :] = base_ref[b, pl.ds(x * Y, Y), :]
        new[c, pl.ds(ROWS + ZERO - 1, X, stride=ROWS), :] = left_ref[Y_BASE + c]
        new[c, pl.ds(ROWS + ZERO + Y, X, stride=ROWS), :] = right_ref[Y_BASE + c]
    odd = index_x % 2 == 1
    for ref, high in ((xa_ref, jnp.logical_not(odd)), (xb_ref, odd)):
        for d in (1, 2):
            x = jnp.where(high, X - 1 + d, -d)
            rows = Y + 2 * (3 - d)
            for c in range(9):
                wide[c, pl.ds((x + 3) * ROWS + ZERO - (3 - d), rows), :] = ref[
                    pl.ds(now_row(c, d), rows), :
                ]
            pert[pl.ds((x + 2) * ROWS + ZERO - (2 - d), rows - 2), :] = ref[
                pl.ds(pert_row(d), rows - 2), :
            ]
            if d == 1:
                for c in range(6):
                    new[c, pl.ds((x + 1) * ROWS + ZERO, Y), :] = ref[pl.ds(X_BASE + c * Y, Y), :]

    def row_mask(first, rows):
        y = lax.broadcasted_iota(jnp.int32, (rows, Z), 0) + first
        return ((y >= 0) | (index_y > 0)) & ((y < Y) | (index_y < last_y))

    def plane_valid(x):
        return ((x >= 0) | (index_x > 0)) & ((x < X) | (index_x < last_x))

    def along_z(value):
        lane = lax.broadcasted_iota(jnp.int32, value.shape, 1)
        after = jnp.where(lane < Z - 1, pltpu.roll(value, Z - 1, 1), 0.0)
        before = jnp.where(lane > 0, pltpu.roll(value, 1, 1), 0.0)
        return after - before

    def differences(ref, c, row, rows):
        return (
            ref[c, pl.ds(row + ROWS, rows), :] - ref[c, pl.ds(row - ROWS, rows), :],
            ref[c, pl.ds(row + 1, rows), :] - ref[c, pl.ds(row - 1, rows), :],
            along_z(ref[c, pl.ds(row, rows), :]),
        )

    wide_mask = row_mask(-2, 24)
    lame_rows = jnp.where(wide_mask, 0.5 * lame_ref[...].reshape(1, Z), 0.0)
    shear_rows = jnp.where(wide_mask, shear_ref[...].reshape(1, Z), 0.0)

    @pl.loop(-2, X + 2, unroll=X + 4)
    def _(x):
        row = (x + 3) * ROWS + ZERO - 2
        out = (x + 2) * ROWS + ZERO - 2
        valid = plane_valid(x)
        lame = jnp.where(valid, lame_rows, 0.0)
        shear = jnp.where(valid, shear_rows, 0.0)
        half_shear = 0.5 * shear
        moved = pert[pl.ds(out, 24), :]
        half_moved = 0.5 * moved
        first = None
        for field in range(3):
            gx, gy, gz = zip(*[differences(wide, 3 * field + i, row, 24) for i in range(3)])
            normal = (gx[0], gy[1], gz[2])
            skew = (gy[0] + gx[1], gz[0] + gx[2], gz[1] + gy[2])
            if field == 0:
                first = (normal, skew)
            volume = lame * (gx[0] + gy[1] + gz[2])
            for i in range(3):
                total = shear * normal[i] + volume
                if field == 1:
                    total = total + moved * first[0][i]
                stress[6 * field + i, pl.ds(out, 24), :] = total
                total = half_shear * skew[i]
                if field == 1:
                    total = total + half_moved * first[1][i]
                stress[6 * field + 3 + i, pl.ds(out, 24), :] = total

    new_mask = row_mask(-1, 24)
    scale_rows = jnp.where(new_mask, 0.05 * buoy_ref[...].reshape(1, Z), 0.0)
    top = lax.broadcasted_iota(jnp.int32, (24, Z), 1) == 0
    point_rows = jnp.where(new_mask, 0.1 * buoy_ref[...].reshape(1, Z), 0.0)
    received_rows = jnp.where(top, point_rows, 0.0)
    point = [point_rows * force_ref[:, i : i + 1] for i in range(3)]
    first_cell = (index_y * Y - 1 + lax.broadcasted_iota(jnp.int32, (24, Z), 0)) * Z
    source_row = cell_ref[...] - first_cell

    @pl.loop(-1, X + 1, unroll=X + 2)
    def _(x):
        row = (x + 2) * ROWS + ZERO - 1
        out = (x + 1) * ROWS + ZERO - 1
        scale = jnp.where(plane_valid(x), scale_rows, 0.0)

        def across_x(c):
            return stress[c, pl.ds(row + ROWS, 24), :] - stress[c, pl.ds(row - ROWS, 24), :]

        def across_y(c):
            return stress[c, pl.ds(row + 1, 24), :] - stress[c, pl.ds(row - 1, 24), :]

        def across_z(c):
            return along_z(stress[c, pl.ds(row, 24), :])

        change = []
        for field in range(3):
            o = 6 * field
            change.append(
                (
                    scale * (across_x(o) + across_y(o + 3) + across_z(o + 4)),
                    scale * (across_x(o + 3) + across_y(o + 1) + across_z(o + 5)),
                    scale * (across_x(o + 4) + across_y(o + 5) + across_z(o + 2)),
                )
            )
        here = source_row == (index_x * X + x) * (count_y * Y * Z)
        for i in range(3):
            new[i, pl.ds(out, 24), :] = new[i, pl.ds(out, 24), :] + (
                change[0][i] + jnp.where(here, point[i], 0.0)
            )
            new[3 + i, pl.ds(out, 24), :] = new[3 + i, pl.ds(out, 24), :] + (
                change[2][i] + received_rows * change[1][i]
            )

        @pl.when((x >= 0) & (x < X))
        def _():
            at = pl.multiple_of(x * Y, Y)
            for i in range(3):
                bnext_ref[i, pl.ds(at, Y), :] = (
                    base_ref[3 + i, pl.ds(at, Y), :] + change[1][i][1 : Y + 1]
                )

    @pl.loop(0, X, unroll=X)
    def _(x):
        row = pl.multiple_of((x + 1) * ROWS + ZERO, 8)
        at = pl.multiple_of(x * Y, Y)
        for i in range(3):
            fnext_ref[i, pl.ds(at, Y), :] = new[i, pl.ds(row, Y), :]
            aprev_ref[i, pl.ds(at, Y), :] = new[3 + i, pl.ds(row, Y), :]
        hx, hy, hz = zip(*[differences(new, i, row, Y) for i in range(3)])
        kx, ky, kz = zip(*[differences(new, 3 + i, row, Y) for i in range(3)])
        normal = hx[0] * kx[0] + hy[1] * ky[1] + hz[2] * kz[2]
        skew = (
            (hy[0] + hx[1]) * (ky[0] + kx[1])
            + (hz[0] + hx[2]) * (kz[0] + kx[2])
            + (hz[1] + hy[2]) * (kz[1] + ky[2])
        )
        hess_ref[pl.ds(at, Y), :] = -0.0125 * (2.0 * normal + skew)


def shape(*dims):
    return jax.ShapeDtypeStruct(dims, F32)


HBM = pl.BlockSpec(memory_space=pltpu.HBM)
VMEM = pl.BlockSpec(memory_space=pltpu.VMEM)


def on_device(
    forward_prev,
    forward_now,
    born_prev,
    born_now,
    adjoint_now,
    adjoint_next,
    shear_pert,
    lame_depth,
    shear_depth,
    buoyancy,
    drm_cells,
    drm_matrix,
    drm_motion,
    source_cell,
    source_force,
):
    assert forward_now.shape == (1, 3, X, Y, Z)
    count_x = lax.axis_size("gx")
    count_y = lax.axis_size("gy")
    events = lax.axis_size("event")
    flat = [
        a.reshape(3, CELLS, Z)
        for a in (forward_prev, forward_now, born_prev, born_now, adjoint_now, adjoint_next)
    ]
    pert = shear_pert.reshape(CELLS, Z)
    lame, shear, buoy = (a.reshape(1, Z) for a in (lame_depth, shear_depth, buoyancy))

    begin_inputs = (
        *flat,
        pert,
        buoy,
        drm_cells.reshape(1, ELEMS),
        drm_matrix.reshape(9, 1, ELEMS),
        drm_motion.reshape(3, 1, ELEMS),
        lame,
        shear,
    )
    low, high = pl.pallas_call(
        begin_kernel,
        out_shape=(shape(Y_PLANES, X, Z), shape(Y_PLANES, X, Z)),
        in_specs=[HBM] * 13,
        out_specs=[VMEM] * 2,
        scratch_shapes=[pltpu.VMEM(a.shape, a.dtype) for a in begin_inputs]
        + [pltpu.SemaphoreType.DMA((13,))],
        compiler_params=pltpu.CompilerParams(vmem_limit_bytes=60 * 2**20),
        name="begin",
    )(*begin_inputs)

    left = lax.ppermute(high, "gy", [(i, i + 1) for i in range(count_y - 1)])
    right = lax.ppermute(low, "gy", [(i + 1, i) for i in range(count_y - 1)])

    base, xa, xb = pl.pallas_call(
        base_kernel,
        out_shape=(shape(9, CELLS, Z), shape(X_ROWS, Z), shape(X_ROWS, Z)),
        in_specs=[VMEM] * 13,
        out_specs=[VMEM] * 3,
        compiler_params=pltpu.CompilerParams(vmem_limit_bytes=16 * 2**20),
        name="base",
    )(*begin_inputs)

    xa, xb = pl.pallas_call(
        widen_kernel,
        out_shape=(shape(X_ROWS, Z), shape(X_ROWS, Z)),
        in_specs=[VMEM] * 4,
        out_specs=[VMEM] * 2,
        compiler_params=pltpu.CompilerParams(vmem_limit_bytes=4 * 2**20),
        name="widen",
    )(xa, xb, left, right)

    def swap(first):
        pairs = []
        for i in range(first, count_x - 1, 2):
            pairs += [(i, i + 1), (i + 1, i)]
        return pairs

    xa = lax.ppermute(xa, "gx", swap(0))
    xb = lax.ppermute(xb, "gx", swap(1))

    hess, forward_next, born_next, adjoint_prev = pl.pallas_call(
        functools.partial(step_kernel, count_x, count_y),
        out_shape=(shape(CELLS, Z), shape(3, CELLS, Z), shape(3, CELLS, Z), shape(3, CELLS, Z)),
        in_specs=[VMEM] * 14,
        out_specs=[VMEM] * 4,
        scratch_shapes=[
            pltpu.VMEM((9, (X + 6) * ROWS, Z), F32),
            pltpu.VMEM(((X + 4) * ROWS, Z), F32),
            pltpu.VMEM((18, (X + 4) * ROWS, Z), F32),
            pltpu.VMEM((6, (X + 2) * ROWS, Z), F32),
        ],
        compiler_params=pltpu.CompilerParams(vmem_limit_bytes=20 * 2**20),
        name="step",
    )(
        flat[1],
        flat[3],
        flat[4],
        pert,
        base,
        left,
        right,
        xa,
        xb,
        lame,
        shear,
        buoy,
        source_cell[:, None] - lax.broadcasted_iota(jnp.int32, (1, Z), 1),
        source_force,
    )

    parts = lax.all_to_all(hess.reshape(events, CELLS // events, Z), "event", 0, 0, tiled=True)
    part = jnp.sum(parts, axis=0)
    spread = jnp.broadcast_to(part[None], (events, CELLS // events, Z))
    hess = lax.all_to_all(spread, "event", 0, 0, tiled=True)

    whole = (1, 3, X, Y, Z)
    return (
        hess.reshape(X, Y, Z),
        forward_next.reshape(whole),
        born_next.reshape(whole),
        adjoint_prev.reshape(whole),
    )


def solution(mesh):
    field = P("event", None, "gx", "gy", None)
    return jax.shard_map(
        on_device,
        mesh=mesh,
        in_specs=(field,) * 6
        + (
            P("gx", "gy", None),
            P(),
            P(),
            P(),
            P("gx", "gy", None),
            P(None, None, "gx", "gy", None),
            P("event", None, "gx", "gy", None),
            P("event"),
            P("event", None),
        ),
        out_specs=(P("gx", "gy", None), field, field, field),
        check_vma=False,
    )
```

```python
import functools

import jax
import jax.numpy as jnp
from jax import lax
from jax.experimental import pallas as pl
from jax.experimental.pallas import tpu as pltpu
from jax.sharding import PartitionSpec as P

X = 16
Y = 16
Z = 128
CELLS = X * Y
LAYER = 4
ELEMS = CELLS * LAYER

Y_BASE = 18
Y_PERT = 24
Y_PLANES = 26

X_STEP = 38
X_PERT = 9 * X_STEP
X_BASE = X_PERT + 34
X_ROWS = X_BASE + 6 * Y

ROWS = 32
ZERO = 8

F32 = jnp.float32


def now_row(c, d):
    return c * X_STEP + (0, 20)[d - 1]


def pert_row(d):
    return X_PERT + (0, 18)[d - 1]


def near_x(high, d):
    return jnp.where(high, X - d, d - 1)


def element_force(depth, matrix_ref, motion_ref):
    slot = lax.broadcasted_iota(jnp.int32, (16, ELEMS), 0)
    spread = jnp.zeros((16, ELEMS), F32)
    for i in range(3):
        element = sum(
            matrix_ref[3 * i + c].reshape(1, ELEMS) * motion_ref[c].reshape(1, ELEMS)
            for c in range(3)
        )
        spread = jnp.where(slot == depth - (Z - 16) - 4 * i, element, spread)
    rest = jnp.concatenate([jnp.zeros((Z - 16, ELEMS), F32), spread], axis=0)
    parts = []
    for _ in range(3):
        parts.append(rest.astype(jnp.bfloat16))
        rest = rest - parts[-1].astype(F32)
    return parts


def placed_force(columns, cells_ref, matrix_ref, motion_ref):
    rows = columns.shape[0]
    cells = cells_ref[...].reshape(1, ELEMS)
    pick = jnp.where(columns == cells // Z, 1.0, 0.0).astype(jnp.bfloat16)
    placed = jnp.zeros((rows, Z), F32)
    for part in element_force(cells % Z, matrix_ref, motion_ref):
        placed = placed + lax.dot_general(
            pick, part, (((1,), (1,)), ((), ())), preferred_element_type=F32
        )
    lane = lax.broadcasted_iota(jnp.int32, (rows, Z), 1)
    applied = []
    for i in range(3):
        moved = placed if i == 0 else pltpu.roll(placed, 4 * i, 1)
        applied.append(jnp.where(lane >= Z - LAYER, moved, 0.0))
    return applied


def edge_coefficients(shear, lame, along):
    return [2.0 * shear + lame if i == along else shear for i in range(3)]


def edge_bases(lame_ref, shear_ref, buoy_ref, along, bases, far, pert):
    scale = 0.1 * buoy_ref[...].reshape(1, Z)
    top = lax.broadcasted_iota(jnp.int32, (1, Z), 1) == 0
    surface_scale = jnp.where(top, scale, 0.0)
    quarter = 0.25 * scale
    coefficients = edge_coefficients(
        quarter * shear_ref[...].reshape(1, Z), quarter * lame_ref[...].reshape(1, Z), along
    )
    forward, adjoint = [], []
    for i in range(3):
        moved = quarter * pert * (2.0 if i == along else 1.0)
        forward.append(bases[0][i] + coefficients[i] * far[0][i])
        born = bases[1][i] + coefficients[i] * far[1][i] + moved * far[0][i]
        adjoint.append(bases[2][i] + coefficients[i] * far[2][i] + surface_scale * born)
    return forward + adjoint


def plane_rows(ref, y):
    return ref[pl.ds(y, X, stride=Y), :]


def begin_kernel(*refs):
    sources, low_ref, high_ref = refs[:13], refs[13], refs[14]
    held, arrived = refs[15:28], refs[28]
    copies = [
        pltpu.make_async_copy(source, ref, arrived.at[i])
        for i, (source, ref) in enumerate(zip(sources, held))
    ]
    order = (8, 9, 10, 1, 3, 4, 6, 7, 11, 12, 0, 2, 5)
    for i in order:
        copies[i].start()
    fprev_ref, fnow_ref, bprev_ref, bnow_ref, anow_ref, anext_ref = held[:6]
    pert_ref, buoy_ref, cells_ref, matrix_ref, motion_ref, lame_ref, shear_ref = held[6:]
    for i in order[:3]:
        copies[i].wait()

    row = lax.broadcasted_iota(jnp.int32, (2 * X, ELEMS), 0)
    columns = (row % X) * Y + jnp.where(row < X, 0, Y - 1)
    applied = placed_force(columns, cells_ref, matrix_ref, motion_ref)

    for i in order[3:9]:
        copies[i].wait()
    now = [r.at[i] for r in (fnow_ref, bnow_ref, anow_ref) for i in range(3)]
    for c in range(9):
        for k in range(2):
            low_ref[2 * c + k] = plane_rows(now[c], k)
            high_ref[2 * c + k] = plane_rows(now[c], Y - 2 + k)
    for k in range(2):
        low_ref[Y_PERT + k] = plane_rows(pert_ref, k)
        high_ref[Y_PERT + k] = plane_rows(pert_ref, Y - 2 + k)

    for i in order[9:]:
        copies[i].wait()
    scale = 0.1 * buoy_ref[...].reshape(1, Z)
    for ref, y, step, first in ((low_ref, 0, 1, 0), (high_ref, Y - 1, -1, X)):
        bases = [
            [2.0 * plane_rows(now[3 * f + i], y) - plane_rows(old.at[i], y) for i in range(3)]
            for f, old in enumerate((fprev_ref, bprev_ref, anext_ref))
        ]
        for i in range(3):
            bases[0][i] = bases[0][i] + scale * applied[i][first : first + X]
        far = [[plane_rows(now[3 * f + i], y + 2 * step) for i in range(3)] for f in range(3)]
        sent = edge_bases(
            lame_ref, shear_ref, buoy_ref, 1, bases, far, plane_rows(pert_ref, y + step)
        )
        for c in range(6):
            ref[Y_BASE + c] = sent[c]


def base_kernel(
    fprev_ref,
    fnow_ref,
    bprev_ref,
    bnow_ref,
    anow_ref,
    anext_ref,
    pert_ref,
    buoy_ref,
    cells_ref,
    matrix_ref,
    motion_ref,
    lame_ref,
    shear_ref,
    base_ref,
    xa_ref,
    xb_ref,
):
    columns = lax.broadcasted_iota(jnp.int32, (CELLS, ELEMS), 0)
    applied = placed_force(columns, cells_ref, matrix_ref, motion_ref)
    scale = 0.1 * buoy_ref[...].reshape(1, Z)
    top = lax.broadcasted_iota(jnp.int32, (1, Z), 1) == 0
    surface_scale = jnp.where(top, scale, 0.0)
    for i in range(3):
        base_ref[i] = 2.0 * fnow_ref[i] - fprev_ref[i] + scale * applied[i]
        born = 2.0 * bnow_ref[i] - bprev_ref[i]
        base_ref[3 + i] = born
        base_ref[6 + i] = 2.0 * anow_ref[i] - anext_ref[i] + surface_scale * born

    now = [r.at[i] for r in (fnow_ref, bnow_ref, anow_ref) for i in range(3)]
    odd = lax.axis_index("gx") % 2 == 1
    for ref, high in ((xa_ref, jnp.logical_not(odd)), (xb_ref, odd)):

        def plane_of(source, d):
            start = pl.multiple_of(near_x(high, d) * Y, Y)
            return source[pl.ds(start, Y), :]

        for c in range(9):
            for d in (1, 2):
                ref[pl.ds(now_row(c, d) + 3 - d, Y), :] = plane_of(now[c], d)
        for d in (1, 2):
            ref[pl.ds(pert_row(d) + 2 - d, Y), :] = plane_of(pert_ref, d)
        bases = [[plane_of(base_ref.at[3 * f + i], 1) for i in range(3)] for f in range(3)]
        for i in range(3):
            bases[2][i] = 2.0 * plane_of(now[6 + i], 1) - plane_of(anext_ref.at[i], 1)
        far = [[plane_of(now[3 * f + i], 3) for i in range(3)] for f in range(3)]
        sent = edge_bases(
            lame_ref, shear_ref, buoy_ref, 0, bases, far, plane_of(pert_ref, 2)
        )
        for c in range(6):
            ref[pl.ds(X_BASE + c * Y, Y), :] = sent[c]


def widen_kernel(xb_in, xa_in, right_ref, left_ref, xb_ref, xa_ref):
    odd = lax.axis_index("gx") % 2 == 1
    for source, ref, high in ((xa_in, xa_ref, jnp.logical_not(odd)), (xb_in, xb_ref, odd)):
        ref[...] = source[...]
        for d in (1, 2):
            x = near_x(high, d)
            for c in range(9):
                start = now_row(c, d)
                for k in range(3 - d):
                    ref[pl.ds(start + k, 1), :] = left_ref[2 * c + d - 1 + k, pl.ds(x, 1), :]
                    ref[pl.ds(start + 19 - d + k, 1), :] = right_ref[2 * c + k, pl.ds(x, 1), :]
        x = near_x(high, 1)
        ref[pl.ds(pert_row(1), 1), :] = left_ref[Y_PERT + 1, pl.ds(x, 1), :]
        ref[pl.ds(pert_row(1) + 17, 1), :] = right_ref[Y_PERT, pl.ds(x, 1), :]


def step_kernel(
    count_x,
    count_y,
    fnow_ref,
    bnow_ref,
    anow_ref,
    pert_in,
    base_ref,
    right_ref,
    left_ref,
    xb_ref,
    xa_ref,
    lame_ref,
    shear_ref,
    buoy_ref,
    cell_ref,
    force_ref,
    hess_ref,
    fnext_ref,
    bnext_ref,
    aprev_ref,
    wide,
    pert,
    stress,
    new,
):
    index_x, index_y = lax.axis_index("gx"), lax.axis_index("gy")
    last_x, last_y = count_x - 1, count_y - 1

    now = [r.at[i] for r in (fnow_ref, bnow_ref, anow_ref) for i in range(3)]
    for c in range(9):
        for x in range(X):
            wide[c, pl.ds((x + 3) * ROWS + ZERO, Y), :] = now[c][pl.ds(x * Y, Y), :]
        for k in range(2):
            wide[c, pl.ds(3 * ROWS + ZERO - 2 + k, X, stride=ROWS), :] = left_ref[2 * c + k]
            wide[c, pl.ds(3 * ROWS + ZERO + Y + k, X, stride=ROWS), :] = right_ref[2 * c + k]
        for row in (ZERO - 3, ZERO + Y + 2):
            wide[c, pl.ds(3 * ROWS + row, X, stride=ROWS), :] = jnp.zeros((X, Z), F32)
        for plane in (0, X + 5):
            wide[c, pl.ds(plane * ROWS + ZERO, Y), :] = jnp.zeros((Y, Z), F32)
    for x in range(X):
        pert[pl.ds((x + 2) * ROWS + ZERO, Y), :] = pert_in[pl.ds(x * Y, Y), :]
    for k in range(2):
        pert[pl.ds(2 * ROWS + ZERO - 2 + k, X, stride=ROWS), :] = left_ref[Y_PERT + k]
        pert[pl.ds(2 * ROWS + ZERO + Y + k, X, stride=ROWS), :] = right_ref[Y_PERT + k]
    for c, b in enumerate((0, 1, 2, 6, 7, 8)):
        for x in range(X):
            new[c, pl.ds((x + 1) * ROWS + ZERO, Y), :] = base_ref[b, pl.ds(x * Y, Y), :]
        new[c, pl.ds(ROWS + ZERO - 1, X, stride=ROWS), :] = left_ref[Y_BASE + c]
        new[c, pl.ds(ROWS + ZERO + Y, X, stride=ROWS), :] = right_ref[Y_BASE + c]
    odd = index_x % 2 == 1
    for ref, high in ((xa_ref, jnp.logical_not(odd)), (xb_ref, odd)):
        for d in (1, 2):
            x = jnp.where(high, X - 1 + d, -d)
            rows = Y + 2 * (3 - d)
            for c in range(9):
                wide[c, pl.ds((x + 3) * ROWS + ZERO - (3 - d), rows), :] = ref[
                    pl.ds(now_row(c, d), rows), :
                ]
            pert[pl.ds((x + 2) * ROWS + ZERO - (2 - d), rows - 2), :] = ref[
                pl.ds(pert_row(d), rows - 2), :
            ]
            if d == 1:
                for c in range(6):
                    new[c, pl.ds((x + 1) * ROWS + ZERO, Y), :] = ref[pl.ds(X_BASE + c * Y, Y), :]

    def row_mask(first, rows):
        y = lax.broadcasted_iota(jnp.int32, (rows, Z), 0) + first
        return ((y >= 0) | (index_y > 0)) & ((y < Y) | (index_y < last_y))

    def plane_valid(x):
        return ((x >= 0) | (index_x > 0)) & ((x < X) | (index_x < last_x))

    def along_z(value):
        lane = lax.broadcasted_iota(jnp.int32, value.shape, 1)
        after = jnp.where(lane < Z - 1, pltpu.roll(value, Z - 1, 1), 0.0)
        before = jnp.where(lane > 0, pltpu.roll(value, 1, 1), 0.0)
        return after - before

    def differences(ref, c, row, rows):
        return (
            ref[c, pl.ds(row + ROWS, rows), :] - ref[c, pl.ds(row - ROWS, rows), :],
            ref[c, pl.ds(row + 1, rows), :] - ref[c, pl.ds(row - 1, rows), :],
            along_z(ref[c, pl.ds(row, rows), :]),
        )

    wide_mask = row_mask(-2, 24)
    lame_rows = jnp.where(wide_mask, 0.5 * lame_ref[...].reshape(1, Z), 0.0)
    shear_rows = jnp.where(wide_mask, shear_ref[...].reshape(1, Z), 0.0)

    @pl.loop(-2, X + 2, unroll=X + 4)
    def _(x):
        row = (x + 3) * ROWS + ZERO - 2
        out = (x + 2) * ROWS + ZERO - 2
        valid = plane_valid(x)
        lame = jnp.where(valid, lame_rows, 0.0)
        shear = jnp.where(valid, shear_rows, 0.0)
        half_shear = 0.5 * shear
        moved = pert[pl.ds(out, 24), :]
        half_moved = 0.5 * moved
        first = None
        for field in range(3):
            gx, gy, gz = zip(*[differences(wide, 3 * field + i, row, 24) for i in range(3)])
            normal = (gx[0], gy[1], gz[2])
            skew = (gy[0] + gx[1], gz[0] + gx[2], gz[1] + gy[2])
            if field == 0:
                first = (normal, skew)
            volume = lame * (gx[0] + gy[1] + gz[2])
            for i in range(3):
                total = shear * normal[i] + volume
                if field == 1:
                    total = total + moved * first[0][i]
                stress[6 * field + i, pl.ds(out, 24), :] = total
                total = half_shear * skew[i]
                if field == 1:
                    total = total + half_moved * first[1][i]
                stress[6 * field + 3 + i, pl.ds(out, 24), :] = total

    new_mask = row_mask(-1, 24)
    scale_rows = jnp.where(new_mask, 0.05 * buoy_ref[...].reshape(1, Z), 0.0)
    top = lax.broadcasted_iota(jnp.int32, (24, Z), 1) == 0
    point_rows = jnp.where(new_mask, 0.1 * buoy_ref[...].reshape(1, Z), 0.0)
    received_rows = jnp.where(top, point_rows, 0.0)
    point = [point_rows * force_ref[:, i : i + 1] for i in range(3)]
    first_cell = (index_y * Y - 1 + lax.broadcasted_iota(jnp.int32, (24, Z), 0)) * Z
    source_row = cell_ref[...] - first_cell

    @pl.loop(-1, X + 1, unroll=X + 2)
    def _(x):
        row = (x + 2) * ROWS + ZERO - 1
        out = (x + 1) * ROWS + ZERO - 1
        scale = jnp.where(plane_valid(x), scale_rows, 0.0)

        def across_x(c):
            return stress[c, pl.ds(row + ROWS, 24), :] - stress[c, pl.ds(row - ROWS, 24), :]

        def across_y(c):
            return stress[c, pl.ds(row + 1, 24), :] - stress[c, pl.ds(row - 1, 24), :]

        def across_z(c):
            return along_z(stress[c, pl.ds(row, 24), :])

        change = []
        for field in range(3):
            o = 6 * field
            change.append(
                (
                    scale * (across_x(o) + across_y(o + 3) + across_z(o + 4)),
                    scale * (across_x(o + 3) + across_y(o + 1) + across_z(o + 5)),
                    scale * (across_x(o + 4) + across_y(o + 5) + across_z(o + 2)),
                )
            )
        here = source_row == (index_x * X + x) * (count_y * Y * Z)
        for i in range(3):
            new[i, pl.ds(out, 24), :] = new[i, pl.ds(out, 24), :] + (
                change[0][i] + jnp.where(here, point[i], 0.0)
            )
            new[3 + i, pl.ds(out, 24), :] = new[3 + i, pl.ds(out, 24), :] + (
                change[2][i] + received_rows * change[1][i]
            )

        @pl.when((x >= 0) & (x < X))
        def _():
            at = pl.multiple_of(x * Y, Y)
            for i in range(3):
                bnext_ref[i, pl.ds(at, Y), :] = (
                    base_ref[3 + i, pl.ds(at, Y), :] + change[1][i][1 : Y + 1]
                )

    @pl.loop(0, X, unroll=X)
    def _(x):
        row = pl.multiple_of((x + 1) * ROWS + ZERO, 8)
        at = pl.multiple_of(x * Y, Y)
        for i in range(3):
            fnext_ref[i, pl.ds(at, Y), :] = new[i, pl.ds(row, Y), :]
            aprev_ref[i, pl.ds(at, Y), :] = new[3 + i, pl.ds(row, Y), :]
        hx, hy, hz = zip(*[differences(new, i, row, Y) for i in range(3)])
        kx, ky, kz = zip(*[differences(new, 3 + i, row, Y) for i in range(3)])
        normal = hx[0] * kx[0] + hy[1] * ky[1] + hz[2] * kz[2]
        skew = (
            (hy[0] + hx[1]) * (ky[0] + kx[1])
            + (hz[0] + hx[2]) * (kz[0] + kx[2])
            + (hz[1] + hy[2]) * (kz[1] + ky[2])
        )
        hess_ref[pl.ds(at, Y), :] = -0.0125 * (2.0 * normal + skew)


def shape(*dims):
    return jax.ShapeDtypeStruct(dims, F32)


HBM = pl.BlockSpec(memory_space=pltpu.HBM)
VMEM = pl.BlockSpec(memory_space=pltpu.VMEM)


def on_device(
    forward_prev,
    forward_now,
    born_prev,
    born_now,
    adjoint_now,
    adjoint_next,
    shear_pert,
    lame_depth,
    shear_depth,
    buoyancy,
    drm_cells,
    drm_matrix,
    drm_motion,
    source_cell,
    source_force,
):
    assert forward_now.shape == (1, 3, X, Y, Z)
    count_x = lax.axis_size("gx")
    count_y = lax.axis_size("gy")
    events = lax.axis_size("event")
    flat = [
        a.reshape(3, CELLS, Z)
        for a in (forward_prev, forward_now, born_prev, born_now, adjoint_now, adjoint_next)
    ]
    pert = shear_pert.reshape(CELLS, Z)
    lame, shear, buoy = (a.reshape(1, Z) for a in (lame_depth, shear_depth, buoyancy))

    begin_inputs = (
        *flat,
        pert,
        buoy,
        drm_cells.reshape(1, ELEMS),
        drm_matrix.reshape(9, 1, ELEMS),
        drm_motion.reshape(3, 1, ELEMS),
        lame,
        shear,
    )
    low, high = pl.pallas_call(
        begin_kernel,
        out_shape=(shape(Y_PLANES, X, Z), shape(Y_PLANES, X, Z)),
        in_specs=[HBM] * 13,
        out_specs=[VMEM] * 2,
        scratch_shapes=[pltpu.VMEM(a.shape, a.dtype) for a in begin_inputs]
        + [pltpu.SemaphoreType.DMA((13,))],
        compiler_params=pltpu.CompilerParams(vmem_limit_bytes=60 * 2**20),
        name="begin",
    )(*begin_inputs)

    right = lax.ppermute(low, "gy", [(i + 1, i) for i in range(count_y - 1)])
    left = lax.ppermute(high, "gy", [(i, i + 1) for i in range(count_y - 1)])

    base, xa, xb = pl.pallas_call(
        base_kernel,
        out_shape=(shape(9, CELLS, Z), shape(X_ROWS, Z), shape(X_ROWS, Z)),
        in_specs=[VMEM] * 13,
        out_specs=[VMEM] * 3,
        compiler_params=pltpu.CompilerParams(vmem_limit_bytes=16 * 2**20),
        name="base",
    )(*begin_inputs)

    xb, xa = pl.pallas_call(
        widen_kernel,
        out_shape=(shape(X_ROWS, Z), shape(X_ROWS, Z)),
        in_specs=[VMEM] * 4,
        out_specs=[VMEM] * 2,
        compiler_params=pltpu.CompilerParams(vmem_limit_bytes=4 * 2**20),
        name="widen",
    )(xb, xa, right, left)

    def swap(first):
        pairs = []
        for i in range(first, count_x - 1, 2):
            pairs += [(i, i + 1), (i + 1, i)]
        return pairs

    xb = lax.ppermute(xb, "gx", swap(1))
    xa = lax.ppermute(xa, "gx", swap(0))

    hess, forward_next, born_next, adjoint_prev = pl.pallas_call(
        functools.partial(step_kernel, count_x, count_y),
        out_shape=(shape(CELLS, Z), shape(3, CELLS, Z), shape(3, CELLS, Z), shape(3, CELLS, Z)),
        in_specs=[VMEM] * 14,
        out_specs=[VMEM] * 4,
        scratch_shapes=[
            pltpu.VMEM((9, (X + 6) * ROWS, Z), F32),
            pltpu.VMEM(((X + 4) * ROWS, Z), F32),
            pltpu.VMEM((18, (X + 4) * ROWS, Z), F32),
            pltpu.VMEM((6, (X + 2) * ROWS, Z), F32),
        ],
        compiler_params=pltpu.CompilerParams(vmem_limit_bytes=20 * 2**20),
        name="step",
    )(
        flat[1],
        flat[3],
        flat[4],
        pert,
        base,
        right,
        left,
        xb,
        xa,
        lame,
        shear,
        buoy,
        source_cell[:, None] - lax.broadcasted_iota(jnp.int32, (1, Z), 1),
        source_force,
    )

    parts = lax.all_to_all(hess.reshape(events, CELLS // events, Z), "event", 0, 0, tiled=True)
    part = jnp.sum(parts, axis=0)
    spread = jnp.broadcast_to(part[None], (events, CELLS // events, Z))
    hess = lax.all_to_all(spread, "event", 0, 0, tiled=True)

    whole = (1, 3, X, Y, Z)
    return (
        hess.reshape(X, Y, Z),
        forward_next.reshape(whole),
        born_next.reshape(whole),
        adjoint_prev.reshape(whole),
    )


def solution(mesh):
    field = P("event", None, "gx", "gy", None)
    return jax.shard_map(
        on_device,
        mesh=mesh,
        in_specs=(field,) * 6
        + (
            P("gx", "gy", None),
            P(),
            P(),
            P(),
            P("gx", "gy", None),
            P(None, None, "gx", "gy", None),
            P("event", None, "gx", "gy", None),
            P("event"),
            P("event", None),
        ),
        out_specs=(P("gx", "gy", None), field, field, field),
        check_vma=False,
    )
```

```python
import functools

import jax
import jax.numpy as jnp
from jax import lax
from jax.experimental import pallas as pl
from jax.experimental.pallas import tpu as pltpu
from jax.sharding import PartitionSpec as P

X = 16
Y = 16
Z = 128
CELLS = X * Y
LAYER = 4
ELEMS = CELLS * LAYER

Y_BASE = 18
Y_PERT = 24
Y_PLANES = 26

X_STEP = 38
X_PERT = 9 * X_STEP
X_BASE = X_PERT + 34
X_ROWS = X_BASE + 6 * Y

ROWS = 32
ZERO = 8

F32 = jnp.float32


def now_row(c, d):
    return c * X_STEP + (0, 20)[d - 1]


def pert_row(d):
    return X_PERT + (0, 18)[d - 1]


def near_x(high, d):
    return jnp.where(high, X - d, d - 1)


def element_force(depth, matrix_ref, motion_ref):
    slot = lax.broadcasted_iota(jnp.int32, (16, ELEMS), 0)
    spread = jnp.zeros((16, ELEMS), F32)
    for i in range(3):
        element = sum(
            matrix_ref[3 * i + c].reshape(1, ELEMS) * motion_ref[c].reshape(1, ELEMS)
            for c in range(3)
        )
        spread = jnp.where(slot == depth - (Z - 16) - 4 * i, element, spread)
    rest = jnp.concatenate([jnp.zeros((Z - 16, ELEMS), F32), spread], axis=0)
    parts = []
    for _ in range(3):
        parts.append(rest.astype(jnp.bfloat16))
        rest = rest - parts[-1].astype(F32)
    return parts


def placed_force(columns, cells_ref, matrix_ref, motion_ref):
    rows = columns.shape[0]
    cells = cells_ref[...].reshape(1, ELEMS)
    pick = jnp.where(columns == cells // Z, 1.0, 0.0).astype(jnp.bfloat16)
    placed = jnp.zeros((rows, Z), F32)
    for part in element_force(cells % Z, matrix_ref, motion_ref):
        placed = placed + lax.dot_general(
            pick, part, (((1,), (1,)), ((), ())), preferred_element_type=F32
        )
    lane = lax.broadcasted_iota(jnp.int32, (rows, Z), 1)
    applied = []
    for i in range(3):
        moved = placed if i == 0 else pltpu.roll(placed, 4 * i, 1)
        applied.append(jnp.where(lane >= Z - LAYER, moved, 0.0))
    return applied


def edge_coefficients(shear, lame, along):
    return [2.0 * shear + lame if i == along else shear for i in range(3)]


def edge_bases(lame_ref, shear_ref, buoy_ref, along, bases, far, pert):
    scale = 0.1 * buoy_ref[...].reshape(1, Z)
    top = lax.broadcasted_iota(jnp.int32, (1, Z), 1) == 0
    surface_scale = jnp.where(top, scale, 0.0)
    quarter = 0.25 * scale
    coefficients = edge_coefficients(
        quarter * shear_ref[...].reshape(1, Z), quarter * lame_ref[...].reshape(1, Z), along
    )
    forward, adjoint = [], []
    for i in range(3):
        moved = quarter * pert * (2.0 if i == along else 1.0)
        forward.append(bases[0][i] + coefficients[i] * far[0][i])
        born = bases[1][i] + coefficients[i] * far[1][i] + moved * far[0][i]
        adjoint.append(bases[2][i] + coefficients[i] * far[2][i] + surface_scale * born)
    return forward + adjoint


def plane_rows(ref, y):
    return ref[pl.ds(y, X, stride=Y), :]


def begin_kernel(*refs):
    sources, low_ref, high_ref = refs[:13], refs[13], refs[14]
    held, arrived = refs[15:28], refs[28]
    copies = [
        pltpu.make_async_copy(source, ref, arrived.at[i])
        for i, (source, ref) in enumerate(zip(sources, held))
    ]
    order = (8, 9, 10, 1, 3, 4, 6, 7, 11, 12, 0, 2, 5)
    for i in order:
        copies[i].start()
    fprev_ref, fnow_ref, bprev_ref, bnow_ref, anow_ref, anext_ref = held[:6]
    pert_ref, buoy_ref, cells_ref, matrix_ref, motion_ref, lame_ref, shear_ref = held[6:]
    for i in order[:3]:
        copies[i].wait()

    row = lax.broadcasted_iota(jnp.int32, (2 * X, ELEMS), 0)
    columns = (row % X) * Y + jnp.where(row < X, 0, Y - 1)
    applied = placed_force(columns, cells_ref, matrix_ref, motion_ref)

    for i in order[3:9]:
        copies[i].wait()
    now = [r.at[i] for r in (fnow_ref, bnow_ref, anow_ref) for i in range(3)]
    for c in range(9):
        for k in range(2):
            low_ref[2 * c + k] = plane_rows(now[c], k)
            high_ref[2 * c + k] = plane_rows(now[c], Y - 2 + k)
    for k in range(2):
        low_ref[Y_PERT + k] = plane_rows(pert_ref, k)
        high_ref[Y_PERT + k] = plane_rows(pert_ref, Y - 2 + k)

    for i in order[9:]:
        copies[i].wait()
    scale = 0.1 * buoy_ref[...].reshape(1, Z)
    for ref, y, step, first in ((low_ref, 0, 1, 0), (high_ref, Y - 1, -1, X)):
        bases = [
            [2.0 * plane_rows(now[3 * f + i], y) - plane_rows(old.at[i], y) for i in range(3)]
            for f, old in enumerate((fprev_ref, bprev_ref, anext_ref))
        ]
        for i in range(3):
            bases[0][i] = bases[0][i] + scale * applied[i][first : first + X]
        far = [[plane_rows(now[3 * f + i], y + 2 * step) for i in range(3)] for f in range(3)]
        sent = edge_bases(
            lame_ref, shear_ref, buoy_ref, 1, bases, far, plane_rows(pert_ref, y + step)
        )
        for c in range(6):
            ref[Y_BASE + c] = sent[c]


def base_kernel(
    fprev_ref,
    fnow_ref,
    bprev_ref,
    bnow_ref,
    anow_ref,
    anext_ref,
    pert_ref,
    buoy_ref,
    cells_ref,
    matrix_ref,
    motion_ref,
    lame_ref,
    shear_ref,
    cell_in,
    base_ref,
    xa_ref,
    xb_ref,
    cell_ref,
):
    cell_ref[...] = cell_in[...]
    columns = lax.broadcasted_iota(jnp.int32, (CELLS, ELEMS), 0)
    applied = placed_force(columns, cells_ref, matrix_ref, motion_ref)
    scale = 0.1 * buoy_ref[...].reshape(1, Z)
    top = lax.broadcasted_iota(jnp.int32, (1, Z), 1) == 0
    surface_scale = jnp.where(top, scale, 0.0)
    for i in range(3):
        base_ref[i] = 2.0 * fnow_ref[i] - fprev_ref[i] + scale * applied[i]
        born = 2.0 * bnow_ref[i] - bprev_ref[i]
        base_ref[3 + i] = born
        base_ref[6 + i] = 2.0 * anow_ref[i] - anext_ref[i] + surface_scale * born

    now = [r.at[i] for r in (fnow_ref, bnow_ref, anow_ref) for i in range(3)]
    odd = lax.axis_index("gx") % 2 == 1
    for ref, high in ((xa_ref, jnp.logical_not(odd)), (xb_ref, odd)):

        def plane_of(source, d):
            start = pl.multiple_of(near_x(high, d) * Y, Y)
            return source[pl.ds(start, Y), :]

        for c in range(9):
            for d in (1, 2):
                ref[pl.ds(now_row(c, d) + 3 - d, Y), :] = plane_of(now[c], d)
        for d in (1, 2):
            ref[pl.ds(pert_row(d) + 2 - d, Y), :] = plane_of(pert_ref, d)
        bases = [[plane_of(base_ref.at[3 * f + i], 1) for i in range(3)] for f in range(3)]
        for i in range(3):
            bases[2][i] = 2.0 * plane_of(now[6 + i], 1) - plane_of(anext_ref.at[i], 1)
        far = [[plane_of(now[3 * f + i], 3) for i in range(3)] for f in range(3)]
        sent = edge_bases(
            lame_ref, shear_ref, buoy_ref, 0, bases, far, plane_of(pert_ref, 2)
        )
        for c in range(6):
            ref[pl.ds(X_BASE + c * Y, Y), :] = sent[c]


def widen_kernel(xb_in, xa_in, right_ref, left_ref, xb_ref, xa_ref):
    odd = lax.axis_index("gx") % 2 == 1
    for source, ref, high in ((xa_in, xa_ref, jnp.logical_not(odd)), (xb_in, xb_ref, odd)):
        ref[...] = source[...]
        for d in (1, 2):
            x = near_x(high, d)
            for c in range(9):
                start = now_row(c, d)
                for k in range(3 - d):
                    ref[pl.ds(start + k, 1), :] = left_ref[2 * c + d - 1 + k, pl.ds(x, 1), :]
                    ref[pl.ds(start + 19 - d + k, 1), :] = right_ref[2 * c + k, pl.ds(x, 1), :]
        x = near_x(high, 1)
        ref[pl.ds(pert_row(1), 1), :] = left_ref[Y_PERT + 1, pl.ds(x, 1), :]
        ref[pl.ds(pert_row(1) + 17, 1), :] = right_ref[Y_PERT, pl.ds(x, 1), :]


INNER = (((1, X - 1),), ((2, X - 2),), ((3, X - 3),))
OUTER = (
    ((-2, 3), (X - 3, X + 2)),
    ((-1, 2), (X - 2, X + 1)),
    ((0, 3), (X - 3, X)),
)


def over(ranges):
    def run(body):
        for low, high in ranges:
            pl.loop(low, high, unroll=high - low)(body)

    return run


def sweep(
    count_x,
    count_y,
    stages,
    base_ref,
    constants,
    state,
    between,
):
    first, second, third = stages
    lame_ref, shear_ref, buoy_ref, cell_ref, force_ref = constants
    wide, pert, new, born, hess_ref, stress = state
    index_x, index_y = lax.axis_index("gx"), lax.axis_index("gy")
    last_x, last_y = count_x - 1, count_y - 1

    def row_mask(first, rows):
        y = lax.broadcasted_iota(jnp.int32, (rows, Z), 0) + first
        return ((y >= 0) | (index_y > 0)) & ((y < Y) | (index_y < last_y))

    def plane_valid(x):
        return ((x >= 0) | (index_x > 0)) & ((x < X) | (index_x < last_x))

    def along_z(value):
        lane = lax.broadcasted_iota(jnp.int32, value.shape, 1)
        after = jnp.where(lane < Z - 1, pltpu.roll(value, Z - 1, 1), 0.0)
        before = jnp.where(lane > 0, pltpu.roll(value, 1, 1), 0.0)
        return after - before

    def differences(ref, c, row, rows):
        return (
            ref[c, pl.ds(row + ROWS, rows), :] - ref[c, pl.ds(row - ROWS, rows), :],
            ref[c, pl.ds(row + 1, rows), :] - ref[c, pl.ds(row - 1, rows), :],
            along_z(ref[c, pl.ds(row, rows), :]),
        )

    wide_mask = row_mask(-2, 24)
    lame_rows = jnp.where(wide_mask, 0.5 * lame_ref[...].reshape(1, Z), 0.0)
    shear_rows = jnp.where(wide_mask, shear_ref[...].reshape(1, Z), 0.0)

    @over(first)
    def _(x):
        row = (x + 3) * ROWS + ZERO - 2
        out = (x + 2) * ROWS + ZERO - 2
        valid = plane_valid(x)
        lame = jnp.where(valid, lame_rows, 0.0)
        shear = jnp.where(valid, shear_rows, 0.0)
        half_shear = 0.5 * shear
        moved = pert[pl.ds(out, 24), :]
        half_moved = 0.5 * moved
        background = None
        for field in range(3):
            gx, gy, gz = zip(*[differences(wide, 3 * field + i, row, 24) for i in range(3)])
            normal = (gx[0], gy[1], gz[2])
            skew = (gy[0] + gx[1], gz[0] + gx[2], gz[1] + gy[2])
            if field == 0:
                background = (normal, skew)
            volume = lame * (gx[0] + gy[1] + gz[2])
            for i in range(3):
                total = shear * normal[i] + volume
                if field == 1:
                    total = total + moved * background[0][i]
                stress[6 * field + i, pl.ds(out, 24), :] = total
                total = half_shear * skew[i]
                if field == 1:
                    total = total + half_moved * background[1][i]
                stress[6 * field + 3 + i, pl.ds(out, 24), :] = total

    new_mask = row_mask(-1, 24)
    scale_rows = jnp.where(new_mask, 0.05 * buoy_ref[...].reshape(1, Z), 0.0)
    top = lax.broadcasted_iota(jnp.int32, (24, Z), 1) == 0
    point_rows = jnp.where(new_mask, 0.1 * buoy_ref[...].reshape(1, Z), 0.0)
    received_rows = jnp.where(top, point_rows, 0.0)
    point = [point_rows * force_ref[:, i : i + 1] for i in range(3)]
    first_cell = (index_y * Y - 1 + lax.broadcasted_iota(jnp.int32, (24, Z), 0)) * Z
    source_row = cell_ref[...] - first_cell

    @over(second)
    def _(x):
        row = (x + 2) * ROWS + ZERO - 1
        out = (x + 1) * ROWS + ZERO - 1
        scale = jnp.where(plane_valid(x), scale_rows, 0.0)

        def across_x(c):
            return stress[c, pl.ds(row + ROWS, 24), :] - stress[c, pl.ds(row - ROWS, 24), :]

        def across_y(c):
            return stress[c, pl.ds(row + 1, 24), :] - stress[c, pl.ds(row - 1, 24), :]

        def across_z(c):
            return along_z(stress[c, pl.ds(row, 24), :])

        change = []
        for field in range(3):
            o = 6 * field
            change.append(
                (
                    scale * (across_x(o) + across_y(o + 3) + across_z(o + 4)),
                    scale * (across_x(o + 3) + across_y(o + 1) + across_z(o + 5)),
                    scale * (across_x(o + 4) + across_y(o + 5) + across_z(o + 2)),
                )
            )
        here = source_row == (index_x * X + x) * (count_y * Y * Z)
        for i in range(3):
            new[i, pl.ds(out, 24), :] = new[i, pl.ds(out, 24), :] + (
                change[0][i] + jnp.where(here, point[i], 0.0)
            )
            new[3 + i, pl.ds(out, 24), :] = new[3 + i, pl.ds(out, 24), :] + (
                change[2][i] + received_rows * change[1][i]
            )

        @pl.when((x >= 0) & (x < X))
        def _():
            at = pl.multiple_of(x * Y, Y)
            for i in range(3):
                born[i, pl.ds(at, Y), :] = (
                    base_ref[3 + i, pl.ds(at, Y), :] + change[1][i][1 : Y + 1]
                )

    between()

    @over(third)
    def _(x):
        row = pl.multiple_of((x + 1) * ROWS + ZERO, 8)
        at = pl.multiple_of(x * Y, Y)
        hx, hy, hz = zip(*[differences(new, i, row, Y) for i in range(3)])
        kx, ky, kz = zip(*[differences(new, 3 + i, row, Y) for i in range(3)])
        normal = hx[0] * kx[0] + hy[1] * ky[1] + hz[2] * kz[2]
        skew = (
            (hy[0] + hx[1]) * (ky[0] + kx[1])
            + (hz[0] + hx[2]) * (kz[0] + kx[2])
            + (hz[1] + hy[2]) * (kz[1] + ky[2])
        )
        hess_ref[pl.ds(at, Y), :] = -0.0125 * (2.0 * normal + skew)


def inner_kernel(
    count_x,
    count_y,
    fnow_ref,
    bnow_ref,
    anow_ref,
    pert_in,
    base_ref,
    right_ref,
    left_ref,
    *refs,
):
    constants, state = refs[:5], refs[5:]
    wide, pert, new, born, hess_ref, stress = state
    now = [r.at[i] for r in (fnow_ref, bnow_ref, anow_ref) for i in range(3)]
    for c in range(9):
        for x in range(X):
            wide[c, pl.ds((x + 3) * ROWS + ZERO, Y), :] = now[c][pl.ds(x * Y, Y), :]
        for k in range(2):
            wide[c, pl.ds(3 * ROWS + ZERO - 2 + k, X, stride=ROWS), :] = left_ref[2 * c + k]
            wide[c, pl.ds(3 * ROWS + ZERO + Y + k, X, stride=ROWS), :] = right_ref[2 * c + k]
        for row in (ZERO - 3, ZERO + Y + 2):
            wide[c, pl.ds(3 * ROWS + row, X, stride=ROWS), :] = jnp.zeros((X, Z), F32)
        for plane in (0, X + 5):
            wide[c, pl.ds(plane * ROWS + ZERO, Y), :] = jnp.zeros((Y, Z), F32)
    for x in range(X):
        pert[pl.ds((x + 2) * ROWS + ZERO, Y), :] = pert_in[pl.ds(x * Y, Y), :]
    for k in range(2):
        pert[pl.ds(2 * ROWS + ZERO - 2 + k, X, stride=ROWS), :] = left_ref[Y_PERT + k]
        pert[pl.ds(2 * ROWS + ZERO + Y + k, X, stride=ROWS), :] = right_ref[Y_PERT + k]
    for c, b in enumerate((0, 1, 2, 6, 7, 8)):
        for x in range(X):
            new[c, pl.ds((x + 1) * ROWS + ZERO, Y), :] = base_ref[b, pl.ds(x * Y, Y), :]
        new[c, pl.ds(ROWS + ZERO - 1, X, stride=ROWS), :] = left_ref[Y_BASE + c]
        new[c, pl.ds(ROWS + ZERO + Y, X, stride=ROWS), :] = right_ref[Y_BASE + c]
    sweep(count_x, count_y, INNER, base_ref, constants, state, lambda: None)


def step_kernel(count_x, count_y, base_ref, xb_ref, xa_ref, *refs):
    constants, refs = refs[:5], refs[10:]
    wide, pert, new, born, hess_ref = refs[:5]
    fnext_ref, bnext_ref, aprev_ref, stress, sent = refs[5:]
    state = (*refs[:5], stress)
    index_x = lax.axis_index("gx")
    odd = index_x % 2 == 1
    for ref, high in ((xa_ref, jnp.logical_not(odd)), (xb_ref, odd)):
        for d in (1, 2):
            x = jnp.where(high, X - 1 + d, -d)
            rows = Y + 2 * (3 - d)
            for c in range(9):
                wide[c, pl.ds((x + 3) * ROWS + ZERO - (3 - d), rows), :] = ref[
                    pl.ds(now_row(c, d), rows), :
                ]
            pert[pl.ds((x + 2) * ROWS + ZERO - (2 - d), rows - 2), :] = ref[
                pl.ds(pert_row(d), rows - 2), :
            ]
            if d == 1:
                for c in range(6):
                    new[c, pl.ds((x + 1) * ROWS + ZERO, Y), :] = ref[pl.ds(X_BASE + c * Y, Y), :]

    inner = new.reshape(6, X + 2, ROWS, Z)
    copies = [
        pltpu.make_async_copy(
            inner.at[pl.ds(first, 3), pl.ds(1, X), pl.ds(ZERO, Y), :], ref, sent.at[k]
        )
        for k, (first, ref) in enumerate(((0, fnext_ref), (3, aprev_ref)))
    ] + [pltpu.make_async_copy(born, bnext_ref, sent.at[2])]

    def send():
        for copy in copies:
            copy.start()

    sweep(count_x, count_y, OUTER, base_ref, constants, state, send)

    for copy in copies:
        copy.wait()


def shape(*dims):
    return jax.ShapeDtypeStruct(dims, F32)


HBM = pl.BlockSpec(memory_space=pltpu.HBM)
VMEM = pl.BlockSpec(memory_space=pltpu.VMEM)


def on_device(
    forward_prev,
    forward_now,
    born_prev,
    born_now,
    adjoint_now,
    adjoint_next,
    shear_pert,
    lame_depth,
    shear_depth,
    buoyancy,
    drm_cells,
    drm_matrix,
    drm_motion,
    source_cell,
    source_force,
):
    assert forward_now.shape == (1, 3, X, Y, Z)
    count_x = lax.axis_size("gx")
    count_y = lax.axis_size("gy")
    events = lax.axis_size("event")
    flat = [
        a.reshape(3, CELLS, Z)
        for a in (forward_prev, forward_now, born_prev, born_now, adjoint_now, adjoint_next)
    ]
    pert = shear_pert.reshape(CELLS, Z)
    lame, shear, buoy = (a.reshape(1, Z) for a in (lame_depth, shear_depth, buoyancy))

    begin_inputs = (
        *flat,
        pert,
        buoy,
        drm_cells.reshape(1, ELEMS),
        drm_matrix.reshape(9, 1, ELEMS),
        drm_motion.reshape(3, 1, ELEMS),
        lame,
        shear,
    )
    low, high = pl.pallas_call(
        begin_kernel,
        out_shape=(shape(Y_PLANES, X, Z), shape(Y_PLANES, X, Z)),
        in_specs=[HBM] * 13,
        out_specs=[VMEM] * 2,
        scratch_shapes=[pltpu.VMEM(a.shape, a.dtype) for a in begin_inputs]
        + [pltpu.SemaphoreType.DMA((13,))],
        compiler_params=pltpu.CompilerParams(vmem_limit_bytes=60 * 2**20),
        name="begin",
    )(*begin_inputs)

    right = lax.ppermute(low, "gy", [(i + 1, i) for i in range(count_y - 1)])
    left = lax.ppermute(high, "gy", [(i, i + 1) for i in range(count_y - 1)])

    base, xa, xb, cell = pl.pallas_call(
        base_kernel,
        out_shape=(
            shape(9, CELLS, Z),
            shape(X_ROWS, Z),
            shape(X_ROWS, Z),
            jax.ShapeDtypeStruct((1, Z), jnp.int32),
        ),
        in_specs=[VMEM] * 14,
        out_specs=[VMEM] * 4,
        compiler_params=pltpu.CompilerParams(vmem_limit_bytes=16 * 2**20),
        name="base",
    )(*begin_inputs, source_cell[:, None] - lax.broadcasted_iota(jnp.int32, (1, Z), 1))

    xb, xa = pl.pallas_call(
        widen_kernel,
        out_shape=(shape(X_ROWS, Z), shape(X_ROWS, Z)),
        in_specs=[VMEM] * 4,
        out_specs=[VMEM] * 2,
        compiler_params=pltpu.CompilerParams(vmem_limit_bytes=4 * 2**20),
        name="widen",
    )(xb, xa, right, left)

    def swap(first):
        pairs = []
        for i in range(first, count_x - 1, 2):
            pairs += [(i, i + 1), (i + 1, i)]
        return pairs

    xb = lax.ppermute(xb, "gx", swap(1))
    xa = lax.ppermute(xa, "gx", swap(0))

    constants = (lame, shear, buoy, cell, source_force)
    held = (
        shape(9, (X + 6) * ROWS, Z),
        shape((X + 4) * ROWS, Z),
        shape(6, (X + 2) * ROWS, Z),
        shape(3, CELLS, Z),
        shape(CELLS, Z),
    )
    state = pl.pallas_call(
        functools.partial(inner_kernel, count_x, count_y),
        out_shape=held,
        in_specs=[VMEM] * 12,
        out_specs=[VMEM] * 5,
        scratch_shapes=[pltpu.VMEM((18, (X + 4) * ROWS, Z), F32)],
        compiler_params=pltpu.CompilerParams(vmem_limit_bytes=24 * 2**20),
        name="inner",
    )(flat[1], flat[3], flat[4], pert, base, right, left, *constants)

    *_, hess, forward_next, born_next, adjoint_prev = pl.pallas_call(
        functools.partial(step_kernel, count_x, count_y),
        out_shape=held + (shape(3, X, Y, Z), shape(3, CELLS, Z), shape(3, X, Y, Z)),
        in_specs=[VMEM] * 13,
        out_specs=[VMEM] * 5 + [HBM] * 3,
        scratch_shapes=[
            pltpu.VMEM((18, (X + 4) * ROWS, Z), F32),
            pltpu.SemaphoreType.DMA((3,)),
        ],
        input_output_aliases={8 + i: i for i in range(5)},
        compiler_params=pltpu.CompilerParams(vmem_limit_bytes=24 * 2**20),
        name="step",
    )(base, xb, xa, *constants, *state)

    parts = lax.all_to_all(hess.reshape(events, CELLS // events, Z), "event", 0, 0, tiled=True)
    part = jnp.sum(parts, axis=0)
    spread = jnp.broadcast_to(part[None], (events, CELLS // events, Z))
    hess = lax.all_to_all(spread, "event", 0, 0, tiled=True)

    whole = (1, 3, X, Y, Z)
    return (
        hess.reshape(X, Y, Z),
        forward_next.reshape(whole),
        born_next.reshape(whole),
        adjoint_prev.reshape(whole),
    )


def solution(mesh):
    field = P("event", None, "gx", "gy", None)
    return jax.shard_map(
        on_device,
        mesh=mesh,
        in_specs=(field,) * 6
        + (
            P("gx", "gy", None),
            P(),
            P(),
            P(),
            P("gx", "gy", None),
            P(None, None, "gx", "gy", None),
            P("event", None, "gx", "gy", None),
            P("event"),
            P("event", None),
        ),
        out_specs=(P("gx", "gy", None), field, field, field),
        check_vma=False,
    )
```
